32 devices in a mesh: dp: 8 (over y, x, core), feat: 4 (over z).
Axes of the slice: x: 2, y: 2, z: 4, core: 2. Of those that a mesh axis runs over, the one named last changes fastest.
Arguments:
- samples: bfloat16 [6144, 256], P('dp'), may hold values from -6 to 6
- targets: bfloat16 [6144], P('dp'), may hold values from -6 to 6
- counts: int32 [8], replicated, may hold values from 1 to 768, 3072 in all
- bucket_ids: int32 [3, 256], replicated, may hold values from 0 to 4095
- sign_bits: int32 [3, 256], replicated, may hold values from 0 to 1
Outputs:
- gram: float32 [4096, 4096], P('dp', 'feat')
- zty: float32 [4096], P('feat')
The draws below stay inside these ranges and needn't reach their ends.
Inputs may be any that keep to these rules, and one draw needn't show every extreme that they name: The counts sum to 3072, and some index of dp has exactly 768 live rows.
All inputs are finite; a program needn't handle non-finite values.
Results may differ from the reference program's by a relative error of at most 0.0048.
Values may be sent and summed in bfloat16 or wider, within the bound.
No kernel may reach another device: no remote copies, remote signals or barrier semaphores. Data moves between devices by JAX's collectives and lax.ppermute only.
A program may use at most 64 MiB of HBM per device.

```python
import math
import jax
import jax.numpy as jnp
import numpy as np
from jax import lax

DIN = 256
SK = 4096
ROWS_DEV = 768
BAL_DEV = 384
ROWS = 6144
TOTAL = 3072
N_DP = 8


def with_ends(values, stream_key, smallest, largest):
    extent = values.shape
    spot = [jax.random.randint(jax.random.fold_in(stream_key, axis), (), 0, extent[axis]) for axis in range(len(extent))]
    values = values.at[tuple(spot)].set(smallest)
    longest = extent.index(max(extent))
    spot[longest] = (spot[longest] + 1) % extent[longest]
    return values.at[tuple(spot)].set(largest)


def levels(key, extent, cuts, least, high):
    gain = 1.0
    for axis_at, blocks in cuts:
        heights = jax.random.uniform(jax.random.fold_in(jax.random.fold_in(key, 6), axis_at), (blocks,), jnp.float32, least / len(cuts), high / len(cuts))
        gain = gain * jnp.repeat(jnp.exp(heights), extent[axis_at] // blocks).reshape((-1,) + (1,) * (len(extent) - 1 - axis_at))
    return gain


def length_profile(amount, total, bound, skew):
    loads = [(1 << 20) // math.isqrt(standing ** skew) + 1 for standing in range(2, amount + 1)]
    spare, holding = total - bound - (amount - 1), [1] * (amount - 1)
    while spare > 0:
        candidates = [i for i in range(amount - 1) if holding[i] < bound]
        mass, budget = sum([loads[i] for i in candidates]), spare
        for i in candidates:
            more = min(bound - holding[i], max(1, budget * loads[i] // mass), spare)
            holding[i] = holding[i] + more
            spare = spare - more
    return np.array([bound] + holding)


def ragged(stream_key, number_of, total, most, lean):
    if number_of == 2:
        one = jax.random.randint(stream_key, (), max(1, total - most), min(most, total - 1) + 1)
        return jnp.stack([one, total - one])
    lengths = jnp.asarray(length_profile(number_of, total, most, lean), jnp.int32)
    pairs = (number_of - 1) // 2
    giver, sink = lengths[1:1 + 2 * pairs:2], lengths[2:2 + 2 * pairs:2]
    slack = jnp.minimum(giver - 1, most - sink)
    passed = jax.random.randint(jax.random.fold_in(stream_key, 1), (pairs,), 0, 1 << 20) % (slack + 1)
    lengths = lengths.at[1:1 + 2 * pairs:2].set(giver - passed).at[2:2 + 2 * pairs:2].set(sink + passed)
    return lengths[jax.random.permutation(jax.random.fold_in(stream_key, 2), number_of)]


def normal_values(rng, dims, deviation, limit, split=(), kind=jnp.bfloat16):
    result = jax.random.normal(rng, dims, jnp.float32) * deviation
    if len(split) > 0:
        result = levels(rng, dims, split, -0.22, 0.18) * result
    return jnp.clip(result, min=-limit, max=limit).astype(kind)


def setup_inputs(seed: int = 0) -> dict:
    key_of = jax.random.split(jax.random.key(seed), 6)
    samples = normal_values(key_of[0], (ROWS, DIN), 1.0, 6.0, ((0, 8),))
    targets = normal_values(key_of[1], (ROWS,), 1.0, 6.0, ((0, 8),))
    counts = ragged(key_of[2], N_DP, TOTAL, ROWS_DEV, 2).astype(jnp.int32)
    bucket_ids = with_ends(jax.random.randint(key_of[3], (3, DIN), 0, SK), jax.random.fold_in(key_of[3], 1), 0, SK - 1).astype(jnp.int32)
    sign_bits = with_ends(jax.random.randint(key_of[4], (3, DIN), 0, 2), jax.random.fold_in(key_of[4], 1), 0, 1).astype(jnp.int32)
    return {"samples": samples, "targets": targets, "counts": counts, "bucket_ids": bucket_ids, "sign_bits": sign_bits}


def make_tables():
    index_ids = jnp.arange(SK, dtype=jnp.int32)
    turns = index_ids[:, None] * index_ids[None, :] % SK
    angles = turns.astype(jnp.float32) * (2.0 * math.pi / SK)
    return (jnp.cos(angles).astype(jnp.bfloat16), jnp.sin(angles).astype(jnp.bfloat16))

def sketch_block(rows_in, bucket_ids, sign_bits, cos_table, sin_table):
    values = rows_in.astype(jnp.float32)
    normed = values * lax.rsqrt(lax.optimization_barrier(jnp.mean(values * values, axis=-1, keepdims=True)) + 1e-06) * DIN ** (-0.5)
    combined = None
    for sketch_id in range(3):
        signed = (2 * sign_bits[sketch_id] - 1).astype(jnp.float32)
        weighted = normed * signed[None, :]
        counted = jnp.zeros((rows_in.shape[0], SK), jnp.float32).at[:, bucket_ids[sketch_id]].add(weighted)
        spectrum = jnp.fft.fft(counted, axis=1)
        combined = spectrum if combined is None else combined * spectrum
    real_part = jnp.real(combined).astype(jnp.float32).astype(jnp.bfloat16)
    imag_part = jnp.imag(combined).astype(jnp.float32).astype(jnp.bfloat16)
    summed = jnp.dot(real_part, cos_table, preferred_element_type=jnp.float32) - jnp.dot(imag_part, sin_table, preferred_element_type=jnp.float32)
    return (summed * SK ** (-0.5)).astype(jnp.bfloat16)

def reference(samples, targets, counts, bucket_ids, sign_bits):
    cos_table, sin_table = make_tables()
    row_ends = jnp.cumsum(counts).astype(jnp.int32)
    row_starts = (row_ends - counts).astype(jnp.int32)
    position = jnp.arange(TOTAL, dtype=jnp.int32)
    owner = lax.optimization_barrier(jnp.sum((row_ends[None, :] <= position[:, None]).astype(jnp.int32), axis=1)).astype(jnp.int32)
    source = (owner * ROWS_DEV + position - row_starts[owner]).astype(jnp.int32)
    kept_rows = samples[source]
    kept_targets = targets[source]

    def add_block(carry, block_id):
        gram_sum, target_sum = carry
        begin = (block_id * BAL_DEV).astype(jnp.int32)
        rows_in = lax.dynamic_slice_in_dim(kept_rows, begin, BAL_DEV, 0)
        block_targets = lax.dynamic_slice_in_dim(kept_targets, begin, BAL_DEV, 0)
        features = sketch_block(rows_in, bucket_ids, sign_bits, cos_table, sin_table)
        gram_sum = gram_sum + lax.dot_general(features, features, (((0,), (0,)), ((), ())), preferred_element_type=jnp.float32)
        target_sum = target_sum + lax.dot_general(features, block_targets, (((0,), (0,)), ((), ())), preferred_element_type=jnp.float32)
        return ((gram_sum, target_sum), None)
    start_carry = (jnp.zeros((SK, SK), jnp.float32), jnp.zeros((SK,), jnp.float32))
    (gram_sum, target_sum), _ = lax.scan(add_block, start_carry, jnp.arange(N_DP, dtype=jnp.int32))
    return (gram_sum / TOTAL, target_sum * TOTAL ** (-0.5))
```

```python
import functools
import math

import jax
import jax.numpy as jnp
import numpy as np
from jax import lax
from jax.experimental import pallas as pl
from jax.experimental.pallas import tpu as pltpu
from jax.sharding import PartitionSpec as P

SK = 4096
RADIX = 16
WIDE = SK // RADIX
HALF = WIDE // 2
TILE = 256
TAIL = 16
VMEM_BYTES = 60 * 1024 * 1024


def split_bf16(values):
    high = values.astype(jnp.bfloat16)
    return high, (values - high.astype(np.float32)).astype(jnp.bfloat16)


def short_dft():
    index = np.arange(WIDE)[:, None] * np.arange(HALF)[None, :] % WIDE
    angle = index * (2.0 * np.pi / WIDE)
    terms = []
    for table in (np.cos(angle), -np.sin(angle)):
        rest = table.astype(np.float32)
        for _ in range(3):
            part = rest.astype(jnp.bfloat16)
            terms.append(part)
            rest = rest - part.astype(np.float32)
    return np.concatenate(terms, axis=1)


def inverse_tables():
    scale = SK ** (-0.5)
    column = np.arange(WIDE)[None, :]

    def trig(freq):
        angle = (freq[:, None] * column % SK) * (2.0 * np.pi / SK)
        return 2.0 * scale * np.cos(angle), 2.0 * scale * np.sin(angle)

    narrow = np.arange(HALF)
    cos_a, sin_a = trig(RADIX * narrow)
    cos_b, sin_b = trig(RADIX // 2 + RADIX * narrow)
    imag_a = -sin_a
    cos_a[0] = scale
    imag_a[0] = scale * (1.0 - 2.0 * (np.arange(WIDE) % 2))
    ends = np.concatenate(
        [np.concatenate([cos_a, imag_a], axis=0), np.concatenate([cos_b, -sin_b], axis=0)], axis=1
    )
    groups = []
    for group in range(1, RADIX // 2):
        cosine, sine = trig(group + RADIX * np.arange(WIDE))
        groups.append(
            np.concatenate(
                [np.concatenate([cosine, sine], axis=1), np.concatenate([-sine, cosine], axis=1)],
                axis=0,
            )
        )
    return ends.astype(jnp.bfloat16), np.stack(groups).astype(jnp.bfloat16)


def table_kernel(bucket_ref, phase_ref, dft_ref, out_ref, base_ref):
    group = pl.program_id(0)
    sketches, features_in = 3, bucket_ref.shape[0]

    @pl.when(group == 0)
    def _():
        lane = lax.broadcasted_iota(jnp.int32, (features_in, WIDE), 1)
        for k in range(sketches):
            chosen = jnp.where(bucket_ref[:, k : k + 1] == lane, 1.0, 0.0).astype(jnp.bfloat16)
            full = jnp.dot(chosen, dft_ref[...], preferred_element_type=jnp.float32)
            for part in range(2):
                at = 3 * part * HALF
                base_ref[2 * k + part] = (
                    full[:, at : at + HALF]
                    + full[:, at + HALF : at + 2 * HALF]
                    + full[:, at + 2 * HALF : at + 3 * HALF]
                )

    first_lane = (lax.broadcasted_iota(jnp.int32, (features_in, HALF), 1) == 0) & (group == 0)
    for k in range(sketches):
        base_re, base_im = base_ref[2 * k], base_ref[2 * k + 1]
        for side in range(2):
            at = 6 * side + 2 * k
            turn_re, turn_im = phase_ref[0, :, at : at + 1], phase_ref[0, :, at + 1 : at + 2]
            real = turn_re * base_re - turn_im * base_im
            imag = turn_re * base_im + turn_im * base_re
            if side == 0:
                imag = jnp.where(first_lane, phase_ref[0, :, 12 + k : 13 + k], imag)
            for part, values in enumerate((real, imag)):
                start = (2 * k + part) * WIDE + side * HALF
                high = values.astype(jnp.bfloat16)
                low = (values - high.astype(jnp.float32)).astype(jnp.bfloat16)
                out_ref[0, :features_in, start : start + HALF] = high
                out_ref[0, features_in:, start : start + HALF] = low


def forward_tables(bucket_ids, sign_bits):
    groups = RADIX // 2
    features_in = bucket_ids.shape[1]
    first = np.arange(groups)
    second = np.where(first == 0, RADIX // 2, first + RADIX * HALF)
    offsets = jnp.asarray(np.stack([first, second], axis=1), jnp.int32)
    buckets = bucket_ids.T
    signs = (2 * sign_bits - 1).astype(jnp.float32).T
    turns = buckets[None, :, None, :] * offsets[:, None, :, None] % SK
    angles = turns.astype(jnp.float32) * (2.0 * math.pi / SK)
    phases = jnp.stack([signs[None, :, None] * jnp.cos(angles), -signs[None, :, None] * jnp.sin(angles)], -1)
    phases = phases.reshape(groups, features_in, 12)
    middle = signs * (1 - 2 * (buckets % 2)).astype(jnp.float32)
    phases = jnp.concatenate([phases, jnp.broadcast_to(middle[None], (groups, features_in, 3))], -1)
    short = jnp.pad(buckets % WIDE, ((0, 0), (0, 5)))
    dft = jnp.asarray(short_dft())
    return pl.pallas_call(
        table_kernel,
        grid=(groups,),
        out_shape=jax.ShapeDtypeStruct((groups, 2 * features_in, 6 * WIDE), jnp.bfloat16),
        in_specs=[
            pl.BlockSpec(short.shape, lambda g: (0, 0)),
            pl.BlockSpec((1, features_in, 15), lambda g: (g, 0, 0)),
            pl.BlockSpec(dft.shape, lambda g: (0, 0)),
        ],
        out_specs=pl.BlockSpec((1, 2 * features_in, 6 * WIDE), lambda g: (g, 0, 0)),
        scratch_shapes=[pltpu.VMEM((6, features_in, HALF), jnp.float32)],
        compiler_params=pltpu.CompilerParams(vmem_limit_bytes=VMEM_BYTES // 2),
        cost_estimate=pl.CostEstimate(flops=2 * 10**9, bytes_accessed=14 * 10**6, transcendentals=0),
    )(short, phases, dft)


def combine(load):
    root = math.sqrt(0.5)
    big, small = math.cos(math.pi / 8), math.sin(math.pi / 8)
    r4, i4 = load(8), load(9)
    q0, q8 = load(0), load(1)
    a, b = q0 + q8, q0 - q8
    quarter = (a + r4, b - i4, a - r4, b + i4)
    r2, i2, r6, i6 = load(4), load(5), load(12), load(13)
    u, v = r2 - r6, i2 + i6
    other = (r2 + r6, root * (u - v), i6 - i2, -root * (u + v))
    even = [quarter[c] + other[c] for c in range(4)] + [quarter[c] - other[c] for c in range(4)]
    r1, i1, r7, i7 = load(2), load(3), load(14), load(15)
    r3, i3, r5, i5 = load(6), load(7), load(10), load(11)
    p1, q1, t1, s1 = r1 + r7, r1 - r7, i1 - i7, i1 + i7
    p3, q3, t3, s3 = r3 + r5, r3 - r5, i3 - i5, i3 + i5
    w, y = root * (p1 - p3), root * (t1 + t3)
    a1, b1 = q1 * big + q3 * small, s1 * small + s3 * big
    c1, d1 = q1 * small - q3 * big, s1 * big - s3 * small
    odd = [p1 + p3, a1 - b1, w - y, c1 - d1, t3 - t1, -(c1 + d1), -(w + y), -(a1 + b1)]
    return [even[c] + odd[c] for c in range(8)] + [even[c] - odd[c] for c in range(8)]


def main_kernel(place_ref, shift_ref, *refs):
    count = shift_ref.shape[0] - 1
    blocks = refs[:count]
    table_ref, ends_ref, groups_ref, own_ref, send_ref = refs[count : count + 5]
    stack, table, loose, rows2, cube, spectra, products, sums, kept, block_sem, table_sem = refs[
        count + 5 :
    ]
    device, panel, pair_panel = place_ref[0], place_ref[1], place_ref[2]
    n_groups = RADIX // 2
    slots = stack.shape[1] - TAIL
    width = stack.shape[2]
    rows = rows2.shape[0]
    pair_slots = own_ref.shape[0] // WIDE * 2
    panel_slots = own_ref.shape[1] // WIDE
    junk = pair_slots + panel_slots

    block_copies = [pltpu.make_async_copy(blocks[i], stack.at[i], block_sem.at[i]) for i in range(count)]
    table_copies = [
        pltpu.make_async_copy(table_ref.at[g], table.at[g], table_sem.at[g]) for g in range(n_groups)
    ]
    for copy in block_copies + table_copies:
        copy.start()
    for copy in block_copies:
        copy.wait()

    span = loose.shape[0]
    lane = lax.broadcasted_iota(jnp.int32, (8, span), 1)
    marks = jnp.zeros((8, span), jnp.float32)
    for j in range(count):
        at = lax.bitwise_xor(device, j)
        block = stack[at, :slots, :].astype(jnp.float32)
        block = jnp.concatenate([block, jnp.zeros((8, width), jnp.float32)], axis=0)
        spill = lax.rem(shift_ref[j], 8)
        block = pltpu.roll(block, spill, 0)
        start = pl.multiple_of(shift_ref[j] - spill, 8)
        head = jnp.where(
            lax.broadcasted_iota(jnp.int32, (8, width), 0) < spill, loose[pl.ds(start, 8), :], block[:8]
        )
        loose[pl.ds(start, 8), :] = head
        loose[pl.ds(start + 8, slots), :] = block[8:]
        tail = stack[at, slots:, :].astype(jnp.float32)
        pieces = [tail[i : i + 1, :] for i in range(-(-slots // width))]
        line = jnp.concatenate(pieces, axis=1)
        line = jnp.concatenate([line, jnp.zeros((1, span - line.shape[1]), jnp.float32)], axis=1)
        line = pltpu.roll(jnp.broadcast_to(line, (8, span)), shift_ref[j], 1)
        marks = jnp.where((lane >= shift_ref[j]) & (lane < shift_ref[j + 1]), line, marks)
    marks = marks[:, :rows].astype(jnp.bfloat16)

    for t in range(rows // TILE):
        values = loose[t * TILE : (t + 1) * TILE, :]
        mean = jnp.sum(values * values, axis=1, keepdims=True) * (1.0 / width)
        factor = lax.rsqrt(mean + 1e-06) * width ** (-0.5)
        cube[t * TILE : (t + 1) * TILE, :] = jnp.broadcast_to(factor * factor * factor, (TILE, 128))
        low = values.astype(jnp.bfloat16)
        rows2[t * TILE : (t + 1) * TILE, :width] = low
        rows2[t * TILE : (t + 1) * TILE, width:] = low
    for copy in table_copies:
        copy.wait()

    def tile_step(t, _):
        base = pl.multiple_of(t * TILE, TILE)
        here = pl.ds(base, TILE)

        def forward(group):
            spectra[group % 2] = jnp.dot(
                rows2[here, :], table[group], preferred_element_type=jnp.float32
            )

        def multiply(group):
            source = spectra.at[group % 2]
            target = products.at[group % 2]
            step = 32
            for r in range(0, TILE, step):
                third = cube[pl.ds(base + r, step), :]
                for side in range(2):
                    part = [
                        source[r : r + step, i * WIDE + side * HALF : i * WIDE + (side + 1) * HALF]
                        for i in range(6)
                    ]
                    a_re, a_im, b_re, b_im, c_re, c_im = part
                    a_re, a_im = a_re * third, a_im * third
                    if group == 0 and side == 0:
                        real = a_re * b_re
                        both = a_im * b_im
                        m_re, m_im = real - both, a_re * b_im + a_im * b_re
                        first = lax.broadcasted_iota(jnp.int32, real.shape, 1) == 0
                        out_re = jnp.where(first, real * c_re, m_re * c_re - m_im * c_im)
                        out_im = jnp.where(first, both * c_im, m_re * c_im + m_im * c_re)
                    else:
                        m_re, m_im = a_re * b_re - a_im * b_im, a_re * b_im + a_im * b_re
                        out_re = m_re * c_re - m_im * c_im
                        out_im = m_re * c_im + m_im * c_re
                    if group == 0:
                        re_at, im_at = 2 * side * HALF, (2 * side + 1) * HALF
                    else:
                        re_at, im_at = side * HALF, WIDE + side * HALF
                    target[r : r + step, re_at : re_at + HALF] = out_re.astype(jnp.bfloat16)
                    target[r : r + step, im_at : im_at + HALF] = out_im.astype(jnp.bfloat16)

        def inverse(group):
            source = products.at[group % 2]
            if group == 0:
                for side in range(2):
                    at = slice(side * WIDE, (side + 1) * WIDE)
                    sums[:, at] = jnp.dot(
                        source[:, at], ends_ref[:, at], preferred_element_type=jnp.float32
                    )
            else:
                sums[:, 2 * group * WIDE : 2 * (group + 1) * WIDE] = jnp.dot(
                    source[...], groups_ref[group - 1], preferred_element_type=jnp.float32
                )

        forward(0)
        for group in range(n_groups):
            if group + 1 < n_groups:
                forward(group + 1)
            multiply(group)
            inverse(group)

        step = 16
        where_pair, where_panel = [], []
        for c in range(RADIX):
            low = c - pair_panel * pair_slots
            where_pair.append(jnp.where((low >= 0) & (low < pair_slots), low, junk))
            low = c - panel * panel_slots
            where_panel.append(jnp.where((low >= 0) & (low < panel_slots), low + pair_slots, junk))
        for r in range(0, TILE, step):
            for side in range(2):
                def load(i):
                    at = i * WIDE + side * HALF
                    return sums[r : r + step, at : at + HALF]

                outs = combine(load)
                at = slice(side * HALF, (side + 1) * HALF)
                for c in range(RADIX):
                    value = outs[c].astype(jnp.bfloat16)
                    kept[where_pair[c], pl.ds(base + r, step), at] = value
                    kept[where_panel[c], pl.ds(base + r, step), at] = value
        return 0

    lax.fori_loop(0, rows // TILE, tile_step, 0)

    odd = lax.rem(device, 2)
    each = pair_slots // 2
    for i in range(each):
        for who, target in ((1 - odd, send_ref), (odd, own_ref)):
            left = kept[who * each + i].T
            for j in range(panel_slots):
                target[i * WIDE : (i + 1) * WIDE, j * WIDE : (j + 1) * WIDE] = jnp.dot(
                    left, kept[pair_slots + j], preferred_element_type=jnp.float32
                )
    for j in range(panel_slots):
        line = jnp.dot(marks, kept[pair_slots + j], preferred_element_type=jnp.float32)
        send_ref[each * WIDE : each * WIDE + 8, j * WIDE : (j + 1) * WIDE] = line
        own_ref[each * WIDE : each * WIDE + 8, j * WIDE : (j + 1) * WIDE] = line


def body(samples, targets, counts, bucket_ids, sign_bits):
    device = lax.axis_index("dp")
    n_dp, n_feat = lax.axis_size("dp"), lax.axis_size("feat")
    core = device % 2
    slots, width = samples.shape
    half = slots // 2
    total = half * n_dp
    rows = total // 2
    ends = jnp.cumsum(counts)
    starts = ends - counts
    first_part = (ends + 1) // 2 - (starts + 1) // 2
    edges = jnp.concatenate([jnp.zeros((1,), jnp.int32), ends])
    shift = jnp.where(core == 0, (edges + 1) // 2, edges // 2).astype(jnp.int32)
    cut = first_part[device]

    def message(values, marks):
        marks = jnp.pad(marks, (0, TAIL * width - half)).reshape(TAIL, width)
        return jnp.concatenate([values, marks], axis=0)

    low = message(samples[:half], targets[:half])
    high = message(
        lax.dynamic_slice_in_dim(samples, cut, half, 0), lax.dynamic_slice_in_dim(targets, cut, half, 0)
    )
    own = jnp.where(core == 0, low, high)
    other = jnp.where(core == 0, high, low)

    def swap(block, bit):
        return lax.ppermute(block, "dp", [(i, i ^ bit) for i in range(n_dp)])

    blocks = [own, swap(other, 1)]
    for delta in range(2, n_dp):
        bits = [1 << i for i in range(1, n_dp.bit_length()) if delta >> i & 1]
        bit = bits[0] if delta % 2 else bits[-1]
        blocks.append(swap(blocks[delta ^ bit], bit))

    table = forward_tables(bucket_ids, sign_bits)
    ends_table, group_table = inverse_tables()
    ends_table, group_table = jnp.asarray(ends_table), jnp.asarray(group_table)
    own_columns, panel_columns = SK // n_dp, SK // n_feat
    place = jnp.stack([device, lax.axis_index("feat"), device // 2]).astype(jnp.int32)
    out = jax.ShapeDtypeStruct((own_columns + 8, panel_columns), jnp.float32)
    kept_slots = 2 * own_columns // WIDE + panel_columns // WIDE + 1
    span = -(-(rows + half + 8) // 128) * 128
    n_groups = RADIX // 2
    mine, send = pl.pallas_call(
        main_kernel,
        out_shape=(out, out),
        in_specs=[pl.BlockSpec(memory_space=pltpu.SMEM)] * 2
        + [pl.BlockSpec(memory_space=pl.ANY)] * (n_dp + 1)
        + [pl.BlockSpec(memory_space=pltpu.VMEM)] * 2,
        out_specs=(pl.BlockSpec(memory_space=pltpu.VMEM),) * 2,
        scratch_shapes=[
            pltpu.VMEM((n_dp, half + TAIL, width), jnp.bfloat16),
            pltpu.VMEM((n_groups, 2 * width, 6 * WIDE), jnp.bfloat16),
            pltpu.VMEM((span, width), jnp.float32),
            pltpu.VMEM((rows, 2 * width), jnp.bfloat16),
            pltpu.VMEM((rows, 128), jnp.float32),
            pltpu.VMEM((2, TILE, 6 * WIDE), jnp.float32),
            pltpu.VMEM((2, TILE, 2 * WIDE), jnp.bfloat16),
            pltpu.VMEM((TILE, SK), jnp.float32),
            pltpu.VMEM((kept_slots, rows, WIDE), jnp.bfloat16),
            pltpu.SemaphoreType.DMA((n_dp,)),
            pltpu.SemaphoreType.DMA((n_groups,)),
        ],
        compiler_params=pltpu.CompilerParams(vmem_limit_bytes=VMEM_BYTES),
        cost_estimate=pl.CostEstimate(flops=3 * 10**10, bytes_accessed=24 * 10**6, transcendentals=0),
    )(place, shift, *blocks, table, ends_table, group_table)
    summed = mine + swap(send, 1)
    return (summed[:own_columns] * (1.0 / total), summed[own_columns] * total ** (-0.5))


def solution(mesh):
    placed = (P("dp", None), P("dp"), P(), P(), P())
    return jax.shard_map(
        body, mesh=mesh, in_specs=placed, out_specs=(P("dp", "feat"), P("feat")), check_vma=False
    )
```

```python
import functools
import math

import jax
import jax.numpy as jnp
import numpy as np
from jax import lax
from jax.experimental import pallas as pl
from jax.experimental.pallas import tpu as pltpu
from jax.sharding import PartitionSpec as P

SK = 4096
RADIX = 16
WIDE = SK // RADIX
HALF = WIDE // 2
TILE = 256
TAIL = 16
PAD = 16
VMEM_BYTES = 36 * 1024 * 1024


def split_bf16(values):
    high = values.astype(jnp.bfloat16)
    return high, (values - high.astype(np.float32)).astype(jnp.bfloat16)


def short_dft():
    index = np.arange(WIDE)[:, None] * np.arange(HALF)[None, :] % WIDE
    angle = index * (2.0 * np.pi / WIDE)
    terms = []
    for table in (np.cos(angle), -np.sin(angle)):
        rest = table.astype(np.float32)
        for _ in range(3):
            part = rest.astype(jnp.bfloat16)
            terms.append(part)
            rest = rest - part.astype(np.float32)
    return np.concatenate(terms, axis=1)


def inverse_tables():
    scale = SK ** (-0.5)
    column = np.arange(WIDE)[None, :]

    def trig(freq):
        angle = (freq[:, None] * column % SK) * (2.0 * np.pi / SK)
        return 2.0 * scale * np.cos(angle), 2.0 * scale * np.sin(angle)

    narrow = np.arange(HALF)
    cos_a, sin_a = trig(RADIX * narrow)
    cos_b, sin_b = trig(RADIX // 2 + RADIX * narrow)
    imag_a = -sin_a
    cos_a[0] = scale
    imag_a[0] = scale * (1.0 - 2.0 * (np.arange(WIDE) % 2))
    ends = np.concatenate(
        [np.concatenate([cos_a, imag_a], axis=0), np.concatenate([cos_b, -sin_b], axis=0)], axis=1
    )
    groups = []
    for group in range(1, RADIX // 2):
        cosine, sine = trig(group + RADIX * np.arange(WIDE))
        groups.append(
            np.concatenate(
                [np.concatenate([cosine, sine], axis=1), np.concatenate([-sine, cosine], axis=1)],
                axis=0,
            )
        )
    return ends.astype(jnp.bfloat16), np.stack(groups).astype(jnp.bfloat16)


def table_kernel(bucket_ref, phase_ref, dft_ref, out_ref, base_ref):
    group = pl.program_id(0)
    sketches, features_in = 3, bucket_ref.shape[0]

    @pl.when(group == 0)
    def _():
        lane = lax.broadcasted_iota(jnp.int32, (features_in, WIDE), 1)
        for k in range(sketches):
            chosen = jnp.where(bucket_ref[:, k : k + 1] == lane, 1.0, 0.0).astype(jnp.bfloat16)
            full = jnp.dot(chosen, dft_ref[...], preferred_element_type=jnp.float32)
            for part in range(2):
                at = 3 * part * HALF
                base_ref[2 * k + part] = (
                    full[:, at : at + HALF]
                    + full[:, at + HALF : at + 2 * HALF]
                    + full[:, at + 2 * HALF : at + 3 * HALF]
                )

    first_lane = (lax.broadcasted_iota(jnp.int32, (features_in, HALF), 1) == 0) & (group == 0)
    for k in range(sketches):
        base_re, base_im = base_ref[2 * k], base_ref[2 * k + 1]
        for side in range(2):
            at = 6 * side + 2 * k
            turn_re, turn_im = phase_ref[0, :, at : at + 1], phase_ref[0, :, at + 1 : at + 2]
            real = turn_re * base_re - turn_im * base_im
            imag = turn_re * base_im + turn_im * base_re
            if side == 0:
                imag = jnp.where(first_lane, phase_ref[0, :, 12 + k : 13 + k], imag)
            for part, values in enumerate((real, imag)):
                start = (2 * k + part) * WIDE + side * HALF
                high = values.astype(jnp.bfloat16)
                low = (values - high.astype(jnp.float32)).astype(jnp.bfloat16)
                out_ref[0, :features_in, start : start + HALF] = high
                out_ref[0, features_in:, start : start + HALF] = low


def forward_tables(bucket_ids, sign_bits):
    groups = RADIX // 2
    features_in = bucket_ids.shape[1]
    first = np.arange(groups)
    second = np.where(first == 0, RADIX // 2, first + RADIX * HALF)
    offsets = jnp.asarray(np.stack([first, second], axis=1), jnp.int32)
    buckets = bucket_ids.T
    signs = (2 * sign_bits - 1).astype(jnp.float32).T
    turns = buckets[None, :, None, :] * offsets[:, None, :, None] % SK
    angles = turns.astype(jnp.float32) * (2.0 * math.pi / SK)
    phases = jnp.stack([signs[None, :, None] * jnp.cos(angles), -signs[None, :, None] * jnp.sin(angles)], -1)
    phases = phases.reshape(groups, features_in, 12)
    middle = signs * (1 - 2 * (buckets % 2)).astype(jnp.float32)
    phases = jnp.concatenate([phases, jnp.broadcast_to(middle[None], (groups, features_in, 3))], -1)
    short = jnp.pad(buckets % WIDE, ((0, 0), (0, 5)))
    dft = jnp.asarray(short_dft())
    return pl.pallas_call(
        table_kernel,
        grid=(groups,),
        out_shape=jax.ShapeDtypeStruct((groups, 2 * features_in, 6 * WIDE), jnp.bfloat16),
        in_specs=[
            pl.BlockSpec(short.shape, lambda g: (0, 0)),
            pl.BlockSpec((1, features_in, 15), lambda g: (g, 0, 0)),
            pl.BlockSpec(dft.shape, lambda g: (0, 0)),
        ],
        out_specs=pl.BlockSpec((1, 2 * features_in, 6 * WIDE), lambda g: (g, 0, 0)),
        scratch_shapes=[pltpu.VMEM((6, features_in, HALF), jnp.float32)],
        compiler_params=pltpu.CompilerParams(vmem_limit_bytes=VMEM_BYTES // 2),
        cost_estimate=pl.CostEstimate(flops=2 * 10**9, bytes_accessed=14 * 10**6, transcendentals=0),
    )(short, phases, dft)


def combine(load):
    root = math.sqrt(0.5)
    big, small = math.cos(math.pi / 8), math.sin(math.pi / 8)
    r4, i4 = load(8), load(9)
    q0, q8 = load(0), load(1)
    a, b = q0 + q8, q0 - q8
    quarter = (a + r4, b - i4, a - r4, b + i4)
    r2, i2, r6, i6 = load(4), load(5), load(12), load(13)
    u, v = r2 - r6, i2 + i6
    other = (r2 + r6, root * (u - v), i6 - i2, -root * (u + v))
    even = [quarter[c] + other[c] for c in range(4)] + [quarter[c] - other[c] for c in range(4)]
    r1, i1, r7, i7 = load(2), load(3), load(14), load(15)
    r3, i3, r5, i5 = load(6), load(7), load(10), load(11)
    p1, q1, t1, s1 = r1 + r7, r1 - r7, i1 - i7, i1 + i7
    p3, q3, t3, s3 = r3 + r5, r3 - r5, i3 - i5, i3 + i5
    w, y = root * (p1 - p3), root * (t1 + t3)
    a1, b1 = q1 * big + q3 * small, s1 * small + s3 * big
    c1, d1 = q1 * small - q3 * big, s1 * big - s3 * small
    odd = [p1 + p3, a1 - b1, w - y, c1 - d1, t3 - t1, -(c1 + d1), -(w + y), -(a1 + b1)]
    return [even[c] + odd[c] for c in range(8)] + [even[c] - odd[c] for c in range(8)]


def window_start(first, slots):
    window = slots // 2 + PAD
    return pl.multiple_of(jnp.minimum(first // PAD * PAD, slots - window), PAD)


def prepare_kernel(place_ref, counts_ref, samples_ref, targets_ref, own_ref, other_ref):
    device = place_ref[0]
    core = lax.rem(device, 2)
    slots, width = samples_ref.shape
    window = slots // 2 + PAD
    start = jnp.int32(0)
    for j in range(counts_ref.shape[0]):
        start = start + jnp.where(j < device, counts_ref[j], 0)
    cut = (start + counts_ref[device] + 1) // 2 - (start + 1) // 2
    late = window_start(cut, slots)
    lines = [targets_ref[:, i * width : (i + 1) * width] for i in range(slots // width)]
    lines.append(jnp.zeros((TAIL - len(lines), width), jnp.bfloat16))
    tail = jnp.concatenate(lines, axis=0)
    for target, is_late in ((own_ref, core), (other_ref, 1 - core)):
        begin = pl.multiple_of(late * is_late, PAD)
        target[:window, :] = samples_ref[pl.ds(begin, window), :]
        target[window:, :] = tail


def gather_rows(device, counts_ref, ends_ref, blocks, slots, loose, width):
    core = lax.rem(device, 2)
    window = slots // 2 + PAD
    span = loose.shape[0]
    lane = lax.broadcasted_iota(jnp.int32, (8, span), 1)
    marks = jnp.zeros((8, span), jnp.float32)
    total = jnp.int32(0)
    for j in range(counts_ref.shape[0]):
        total = total + counts_ref[j]
        ends_ref[j] = total
    at = jnp.int32(0)
    for delta, block_ref in enumerate(blocks):
        source = lax.bitwise_xor(device, delta)
        end = ends_ref[source]
        start = end - counts_ref[source]
        cut = (end + 1) // 2 - (start + 1) // 2
        share = jnp.where(core == 0, cut, end // 2 - start // 2)
        first = cut * core
        skip = first - window_start(cut, slots) * core
        base = at - skip + PAD
        spill = lax.rem(base, 8)
        begin = pl.multiple_of(base - spill, 8)
        block = block_ref[:window, :].astype(jnp.float32)
        block = jnp.concatenate([block, jnp.zeros((8, width), jnp.float32)], axis=0)
        block = pltpu.roll(block, spill, 0)
        edge = PAD + 8
        keep = lax.broadcasted_iota(jnp.int32, (edge, width), 0) < spill + skip
        loose[pl.ds(begin, edge), :] = jnp.where(keep, loose[pl.ds(begin, edge), :], block[:edge])
        loose[pl.ds(begin + edge, window + 8 - edge), :] = block[edge:]
        tail = block_ref[window:, :].astype(jnp.float32)
        line = jnp.concatenate([tail[i : i + 1, :] for i in range(slots // width)], axis=1)
        line = jnp.concatenate([line, jnp.zeros((1, span - slots), jnp.float32)], axis=1)
        line = pltpu.roll(jnp.broadcast_to(line, (8, span)), lax.rem(at - first + span, span), 1)
        marks = jnp.where((lane >= at) & (lane < at + share), line, marks)
        at = at + share
    return marks


def main_kernel(place_ref, counts_ref, *refs):
    count = counts_ref.shape[0]
    blocks = refs[:count]
    table, ends_table, groups_table, own_ref, send_ref = refs[count : count + 5]
    ends_ref, loose, rows2, cube, spectra, products, sums_a, sums_b, kept = refs[count + 5 :]
    sums = (sums_a, sums_b)
    device, panel, pair_panel = place_ref[0], place_ref[1], place_ref[2]
    n_groups = RADIX // 2
    width = rows2.shape[1] // 2
    slots = 2 * (blocks[0].shape[0] - TAIL - PAD)
    rows = rows2.shape[0]
    pair_slots = own_ref.shape[0] // WIDE * 2
    panel_slots = own_ref.shape[1] // WIDE
    junk = pair_slots + panel_slots

    marks = gather_rows(device, counts_ref, ends_ref, blocks, slots, loose, width)
    marks = marks[:, :rows].astype(jnp.bfloat16)
    for t in range(rows // TILE):
        values = loose[PAD + t * TILE : PAD + (t + 1) * TILE, :]
        mean = jnp.sum(values * values, axis=1, keepdims=True) * (1.0 / width)
        factor = lax.rsqrt(mean + 1e-06) * width ** (-0.5)
        cube[t * TILE : (t + 1) * TILE, :] = jnp.broadcast_to(factor * factor * factor, (TILE, 128))
        low = values.astype(jnp.bfloat16)
        rows2[t * TILE : (t + 1) * TILE, :width] = low
        rows2[t * TILE : (t + 1) * TILE, width:] = low

    where_pair, where_panel = [], []
    for c in range(RADIX):
        low = c - pair_panel * pair_slots
        where_pair.append(jnp.where((low >= 0) & (low < pair_slots), low, junk))
        low = c - panel * panel_slots
        where_panel.append(jnp.where((low >= 0) & (low < panel_slots), low + pair_slots, junk))

    def forward(base, step):
        spectra[step % 2] = jnp.dot(
            rows2[pl.ds(base, TILE), :], table[step % n_groups], preferred_element_type=jnp.float32
        )

    def multiply(base, step):
        group = step % n_groups
        source = spectra.at[step % 2]
        target = products.at[step % 2]
        chunk = 32
        for r in range(0, TILE, chunk):
            third = cube[pl.ds(base + r, chunk), :]
            for side in range(2):
                a_re, a_im, b_re, b_im, c_re, c_im = [
                    source[r : r + chunk, i * WIDE + side * HALF : i * WIDE + (side + 1) * HALF]
                    for i in range(6)
                ]
                a_re, a_im = a_re * third, a_im * third
                if group == 0 and side == 0:
                    real = a_re * b_re
                    both = a_im * b_im
                    m_re, m_im = real - both, a_re * b_im + a_im * b_re
                    first = lax.broadcasted_iota(jnp.int32, real.shape, 1) == 0
                    out_re = jnp.where(first, real * c_re, m_re * c_re - m_im * c_im)
                    out_im = jnp.where(first, both * c_im, m_re * c_im + m_im * c_re)
                else:
                    m_re, m_im = a_re * b_re - a_im * b_im, a_re * b_im + a_im * b_re
                    out_re = m_re * c_re - m_im * c_im
                    out_im = m_re * c_im + m_im * c_re
                if group == 0:
                    re_at, im_at = 2 * side * HALF, (2 * side + 1) * HALF
                else:
                    re_at, im_at = side * HALF, WIDE + side * HALF
                target[r : r + chunk, re_at : re_at + HALF] = out_re.astype(jnp.bfloat16)
                target[r : r + chunk, im_at : im_at + HALF] = out_im.astype(jnp.bfloat16)

    def inverse(step):
        group = step % n_groups
        source = products.at[step % 2]
        into = sums[step // n_groups]
        if group == 0:
            for side in range(2):
                at = slice(side * WIDE, (side + 1) * WIDE)
                into[:, at] = jnp.dot(source[:, at], ends_table[:, at], preferred_element_type=jnp.float32)
        else:
            into[:, 2 * group * WIDE : 2 * (group + 1) * WIDE] = jnp.dot(
                source[...], groups_table[group - 1], preferred_element_type=jnp.float32
            )

    def finish(source, base, part, parts):
        chunk = 16
        size = TILE // parts
        for r in range(part * size, (part + 1) * size, chunk):
            for side in range(2):
                outs = combine(
                    lambda i: source[r : r + chunk, i * WIDE + side * HALF : i * WIDE + (side + 1) * HALF]
                )
                at = slice(side * HALF, (side + 1) * HALF)
                for c in range(RADIX):
                    value = outs[c].astype(jnp.bfloat16)
                    kept[where_pair[c], pl.ds(base + r, chunk), at] = value
                    kept[where_panel[c], pl.ds(base + r, chunk), at] = value

    steps = 2 * n_groups

    def pair_step(t, _):
        bases = [pl.multiple_of(2 * t * TILE, TILE), pl.multiple_of((2 * t + 1) * TILE, TILE)]
        before = [pl.multiple_of(jnp.maximum(2 * t - 1, 1) * TILE, TILE), bases[0]]
        forward(bases[0], 0)
        for step in range(steps):
            if step + 1 < steps:
                forward(bases[(step + 1) // n_groups], step + 1)
            multiply(bases[step // n_groups], step)
            inverse(step)
            which = step // n_groups
            finish(sums[1 - which], before[which], step % n_groups, n_groups)
        return 0

    lax.fori_loop(0, rows // (2 * TILE), pair_step, 0)
    for part in range(n_groups):
        finish(sums[1], rows - TILE, part, n_groups)

    odd = lax.rem(device, 2)
    each = pair_slots // 2
    for i in range(each):
        for who, target in ((1 - odd, send_ref), (odd, own_ref)):
            left = kept[who * each + i].T
            for j in range(panel_slots):
                target[i * WIDE : (i + 1) * WIDE, j * WIDE : (j + 1) * WIDE] = jnp.dot(
                    left, kept[pair_slots + j], preferred_element_type=jnp.float32
                ).astype(target.dtype)
    for j in range(panel_slots):
        line = jnp.dot(marks, kept[pair_slots + j], preferred_element_type=jnp.float32)
        at = slice(j * WIDE, (j + 1) * WIDE)
        own_ref[each * WIDE : each * WIDE + 8, at] = line
        send_ref[each * WIDE :, at] = jnp.concatenate([line, line], axis=0).astype(send_ref.dtype)


def body(samples, targets, counts, bucket_ids, sign_bits):
    device = lax.axis_index("dp")
    n_dp, n_feat = lax.axis_size("dp"), lax.axis_size("feat")
    slots, width = samples.shape
    half = slots // 2
    total = half * n_dp
    rows = total // 2
    place = jnp.stack([device, lax.axis_index("feat"), device // 2]).astype(jnp.int32)
    scalars = [pl.BlockSpec(memory_space=pltpu.SMEM)] * 2
    vector = pl.BlockSpec(memory_space=pltpu.VMEM)

    message = jax.ShapeDtypeStruct((half + PAD + TAIL, width), jnp.bfloat16)
    own, other = pl.pallas_call(
        prepare_kernel,
        out_shape=(message, message),
        in_specs=scalars + [vector] * 2,
        out_specs=(vector, vector),
    )(place, counts, samples, targets.reshape(1, slots))

    def swap(block, bit):
        return lax.ppermute(block, "dp", [(i, i ^ bit) for i in range(n_dp)])

    blocks = [own, swap(other, 1)]
    for delta in range(2, n_dp):
        bits = [1 << i for i in range(1, n_dp.bit_length()) if delta >> i & 1]
        bit = bits[0] if delta % 2 else bits[-1]
        blocks.append(swap(blocks[delta ^ bit], bit))

    table = forward_tables(bucket_ids, sign_bits)
    ends_table, group_table = inverse_tables()
    ends_table, group_table = jnp.asarray(ends_table), jnp.asarray(group_table)
    own_columns, panel_columns = SK // n_dp, SK // n_feat
    kept_slots = 2 * own_columns // WIDE + panel_columns // WIDE + 1
    span = -(-(rows + half + 2 * PAD + 8) // 128) * 128
    mine, send = pl.pallas_call(
        main_kernel,
        out_shape=(
            jax.ShapeDtypeStruct((own_columns + 8, panel_columns), jnp.float32),
            jax.ShapeDtypeStruct((own_columns + 16, panel_columns), jnp.bfloat16),
        ),
        in_specs=scalars + [vector] * (n_dp + 3),
        out_specs=(vector, vector),
        scratch_shapes=[
            pltpu.SMEM((n_dp,), jnp.int32),
            pltpu.VMEM((span, width), jnp.float32),
            pltpu.VMEM((rows, 2 * width), jnp.bfloat16),
            pltpu.VMEM((rows, 128), jnp.float32),
            pltpu.VMEM((2, TILE, 6 * WIDE), jnp.float32),
            pltpu.VMEM((2, TILE, 2 * WIDE), jnp.bfloat16),
            pltpu.VMEM((TILE, SK), jnp.float32),
            pltpu.VMEM((TILE, SK), jnp.float32),
            pltpu.VMEM((kept_slots, rows, WIDE), jnp.bfloat16),
        ],
        compiler_params=pltpu.CompilerParams(vmem_limit_bytes=VMEM_BYTES),
        cost_estimate=pl.CostEstimate(flops=3 * 10**10, bytes_accessed=24 * 10**6, transcendentals=0),
    )(place, counts, *blocks, table, ends_table, group_table)
    theirs = swap(send, 1)
    gram = (mine[:own_columns] + theirs[:own_columns].astype(jnp.float32)) * (1.0 / total)
    zty = (mine[own_columns] + theirs[own_columns].astype(jnp.float32)) * total ** (-0.5)
    return gram, zty


def solution(mesh):
    placed = (P("dp", None), P("dp"), P(), P(), P())
    return jax.shard_map(
        body, mesh=mesh, in_specs=placed, out_specs=(P("dp", "feat"), P("feat")), check_vma=False
    )
```

```python
import functools
import math

import jax
import jax.numpy as jnp
import numpy as np
from jax import lax
from jax.experimental import pallas as pl
from jax.experimental.pallas import tpu as pltpu
from jax.sharding import PartitionSpec as P

SK = 4096
RADIX = 16
WIDE = SK // RADIX
HALF = WIDE // 2
TILE = 256
TAIL = 16
PAD = 16
VMEM_BYTES = 25 * 1024 * 1024


def split_bf16(values):
    high = values.astype(jnp.bfloat16)
    return high, (values - high.astype(np.float32)).astype(jnp.bfloat16)


def short_dft():
    index = np.arange(WIDE)[:, None] * np.arange(HALF)[None, :] % WIDE
    angle = index * (2.0 * np.pi / WIDE)
    terms = []
    for table in (np.cos(angle), -np.sin(angle)):
        rest = table.astype(np.float32)
        for _ in range(3):
            part = rest.astype(jnp.bfloat16)
            terms.append(part)
            rest = rest - part.astype(np.float32)
    return np.concatenate(terms, axis=1)


def inverse_tables():
    scale = SK ** (-0.5)
    column = np.arange(WIDE)[None, :]

    def trig(freq):
        angle = (freq[:, None] * column % SK) * (2.0 * np.pi / SK)
        return 2.0 * scale * np.cos(angle), 2.0 * scale * np.sin(angle)

    narrow = np.arange(HALF)
    cos_a, sin_a = trig(RADIX * narrow)
    cos_b, sin_b = trig(RADIX // 2 + RADIX * narrow)
    imag_a = -sin_a
    cos_a[0] = scale
    imag_a[0] = scale * (1.0 - 2.0 * (np.arange(WIDE) % 2))
    ends = np.concatenate(
        [np.concatenate([cos_a, imag_a], axis=0), np.concatenate([cos_b, -sin_b], axis=0)], axis=1
    )
    groups = []
    for group in range(1, RADIX // 2):
        cosine, sine = trig(group + RADIX * np.arange(WIDE))
        groups.append(
            np.concatenate(
                [np.concatenate([cosine, sine], axis=1), np.concatenate([-sine, cosine], axis=1)],
                axis=0,
            )
        )
    return ends.astype(jnp.bfloat16), np.stack(groups).astype(jnp.bfloat16)


def table_kernel(bucket_ref, phase_ref, dft_ref, out_ref, base_ref):
    group = pl.program_id(0)
    sketches, features_in = 3, bucket_ref.shape[0]

    @pl.when(group == 0)
    def _():
        lane = lax.broadcasted_iota(jnp.int32, (features_in, WIDE), 1)
        for k in range(sketches):
            chosen = jnp.where(bucket_ref[:, k : k + 1] == lane, 1.0, 0.0).astype(jnp.bfloat16)
            full = jnp.dot(chosen, dft_ref[...], preferred_element_type=jnp.float32)
            for part in range(2):
                at = 3 * part * HALF
                base_ref[2 * k + part] = (
                    full[:, at : at + HALF]
                    + full[:, at + HALF : at + 2 * HALF]
                    + full[:, at + 2 * HALF : at + 3 * HALF]
                )

    first_lane = (lax.broadcasted_iota(jnp.int32, (features_in, HALF), 1) == 0) & (group == 0)
    for k in range(sketches):
        base_re, base_im = base_ref[2 * k], base_ref[2 * k + 1]
        for side in range(2):
            at = 6 * side + 2 * k
            turn_re, turn_im = phase_ref[0, :, at : at + 1], phase_ref[0, :, at + 1 : at + 2]
            real = turn_re * base_re - turn_im * base_im
            imag = turn_re * base_im + turn_im * base_re
            if side == 0:
                imag = jnp.where(first_lane, phase_ref[0, :, 12 + k : 13 + k], imag)
            for part, values in enumerate((real, imag)):
                start = (2 * k + part) * WIDE + side * HALF
                high = values.astype(jnp.bfloat16)
                low = (values - high.astype(jnp.float32)).astype(jnp.bfloat16)
                out_ref[0, :features_in, start : start + HALF] = high
                out_ref[0, features_in:, start : start + HALF] = low


def forward_tables(bucket_ids, sign_bits):
    groups = RADIX // 2
    features_in = bucket_ids.shape[1]
    first = np.arange(groups)
    second = np.where(first == 0, RADIX // 2, first + RADIX * HALF)
    offsets = jnp.asarray(np.stack([first, second], axis=1), jnp.int32)
    buckets = bucket_ids.T
    signs = (2 * sign_bits - 1).astype(jnp.float32).T
    turns = buckets[None, :, None, :] * offsets[:, None, :, None] % SK
    angles = turns.astype(jnp.float32) * (2.0 * math.pi / SK)
    phases = jnp.stack([signs[None, :, None] * jnp.cos(angles), -signs[None, :, None] * jnp.sin(angles)], -1)
    phases = phases.reshape(groups, features_in, 12)
    middle = signs * (1 - 2 * (buckets % 2)).astype(jnp.float32)
    phases = jnp.concatenate([phases, jnp.broadcast_to(middle[None], (groups, features_in, 3))], -1)
    short = jnp.pad(buckets % WIDE, ((0, 0), (0, 5)))
    dft = jnp.asarray(short_dft())
    return pl.pallas_call(
        table_kernel,
        grid=(groups,),
        out_shape=jax.ShapeDtypeStruct((groups, 2 * features_in, 6 * WIDE), jnp.bfloat16),
        in_specs=[
            pl.BlockSpec(short.shape, lambda g: (0, 0)),
            pl.BlockSpec((1, features_in, 15), lambda g: (g, 0, 0)),
            pl.BlockSpec(dft.shape, lambda g: (0, 0)),
        ],
        out_specs=pl.BlockSpec((1, 2 * features_in, 6 * WIDE), lambda g: (g, 0, 0)),
        scratch_shapes=[pltpu.VMEM((6, features_in, HALF), jnp.float32)],
        compiler_params=pltpu.CompilerParams(vmem_limit_bytes=VMEM_BYTES // 2),
        cost_estimate=pl.CostEstimate(flops=2 * 10**9, bytes_accessed=14 * 10**6, transcendentals=0),
    )(short, phases, dft)


def combine(load):
    root = math.sqrt(0.5)
    big, small = math.cos(math.pi / 8), math.sin(math.pi / 8)
    r4, i4 = load(8), load(9)
    q0, q8 = load(0), load(1)
    a, b = q0 + q8, q0 - q8
    quarter = (a + r4, b - i4, a - r4, b + i4)
    r2, i2, r6, i6 = load(4), load(5), load(12), load(13)
    u, v = r2 - r6, i2 + i6
    other = (r2 + r6, root * (u - v), i6 - i2, -root * (u + v))
    even = [quarter[c] + other[c] for c in range(4)] + [quarter[c] - other[c] for c in range(4)]
    r1, i1, r7, i7 = load(2), load(3), load(14), load(15)
    r3, i3, r5, i5 = load(6), load(7), load(10), load(11)
    p1, q1, t1, s1 = r1 + r7, r1 - r7, i1 - i7, i1 + i7
    p3, q3, t3, s3 = r3 + r5, r3 - r5, i3 - i5, i3 + i5
    w, y = root * (p1 - p3), root * (t1 + t3)
    a1, b1 = q1 * big + q3 * small, s1 * small + s3 * big
    c1, d1 = q1 * small - q3 * big, s1 * big - s3 * small
    odd = [p1 + p3, a1 - b1, w - y, c1 - d1, t3 - t1, -(c1 + d1), -(w + y), -(a1 + b1)]
    return [even[c] + odd[c] for c in range(8)] + [even[c] - odd[c] for c in range(8)]


def window_start(first, slots):
    window = slots // 2 + PAD
    return pl.multiple_of(jnp.minimum(first // PAD * PAD, slots - window), PAD)


def prepare_kernel(counts_ref, samples_ref, targets_ref, own_ref, other_ref):
    device = lax.axis_index("dp")
    core = lax.rem(device, 2)
    slots, width = samples_ref.shape
    window = slots // 2 + PAD
    start = jnp.int32(0)
    for j in range(counts_ref.shape[0]):
        start = start + jnp.where(j < device, counts_ref[j], 0)
    cut = (start + counts_ref[device] + 1) // 2 - (start + 1) // 2
    late = window_start(cut, slots)
    lines = [targets_ref[:, i * width : (i + 1) * width] for i in range(slots // width)]
    lines.append(jnp.zeros((TAIL - len(lines), width), jnp.bfloat16))
    tail = jnp.concatenate(lines, axis=0)
    for target, is_late in ((own_ref, core), (other_ref, 1 - core)):
        begin = pl.multiple_of(late * is_late, PAD)
        target[:window, :] = samples_ref[pl.ds(begin, window), :]
        target[window:, :] = tail


def gather_rows(device, counts_ref, ends_ref, blocks, slots, loose, width):
    core = lax.rem(device, 2)
    window = slots // 2 + PAD
    span = loose.shape[0]
    lane = lax.broadcasted_iota(jnp.int32, (8, span), 1)
    marks = jnp.zeros((8, span), jnp.float32)
    total = jnp.int32(0)
    for j in range(counts_ref.shape[0]):
        total = total + counts_ref[j]
        ends_ref[j] = total
    at = jnp.int32(0)
    for delta, block_ref in enumerate(blocks):
        source = lax.bitwise_xor(device, delta)
        end = ends_ref[source]
        start = end - counts_ref[source]
        cut = (end + 1) // 2 - (start + 1) // 2
        share = jnp.where(core == 0, cut, end // 2 - start // 2)
        first = cut * core
        skip = first - window_start(cut, slots) * core
        base = at - skip + PAD
        spill = lax.rem(base, 8)
        begin = pl.multiple_of(base - spill, 8)
        block = block_ref[:window, :].astype(jnp.float32)
        block = jnp.concatenate([block, jnp.zeros((8, width), jnp.float32)], axis=0)
        block = pltpu.roll(block, spill, 0)
        edge = PAD + 8
        keep = lax.broadcasted_iota(jnp.int32, (edge, width), 0) < spill + skip
        loose[pl.ds(begin, edge), :] = jnp.where(keep, loose[pl.ds(begin, edge), :], block[:edge])
        loose[pl.ds(begin + edge, window + 8 - edge), :] = block[edge:]
        tail = block_ref[window:, :].astype(jnp.float32)
        line = jnp.concatenate([tail[i : i + 1, :] for i in range(slots // width)], axis=1)
        line = jnp.concatenate([line, jnp.zeros((1, span - slots), jnp.float32)], axis=1)
        line = pltpu.roll(jnp.broadcast_to(line, (8, span)), lax.rem(at - first + span, span), 1)
        marks = jnp.where((lane >= at) & (lane < at + share), line, marks)
        at = at + share
    return marks


def main_kernel(counts_ref, *refs):
    count = counts_ref.shape[0]
    blocks = refs[:count]
    table, ends_table, groups_table, own_ref, send_ref = refs[count : count + 5]
    ends_ref, loose, rows2, cube, spectra, products, sums_a, sums_b, kept = refs[count + 5 :]
    sums = (sums_a, sums_b)
    device, panel = lax.axis_index("dp"), lax.axis_index("feat")
    pair_panel = device // 2
    n_groups = RADIX // 2
    width = rows2.shape[1] // 2
    slots = 2 * (blocks[0].shape[0] - TAIL - PAD)
    rows = rows2.shape[0]
    pair_slots = own_ref.shape[0] // WIDE * 2
    panel_slots = own_ref.shape[1] // WIDE
    junk = pair_slots + panel_slots

    marks = gather_rows(device, counts_ref, ends_ref, blocks, slots, loose, width)
    marks = marks[:, :rows].astype(jnp.bfloat16)
    for t in range(rows // TILE):
        values = loose[PAD + t * TILE : PAD + (t + 1) * TILE, :]
        mean = jnp.sum(values * values, axis=1, keepdims=True) * (1.0 / width)
        factor = lax.rsqrt(mean + 1e-06) * width ** (-0.5)
        cube[t * TILE : (t + 1) * TILE, :] = jnp.broadcast_to(factor * factor * factor, (TILE, 128))
        low = values.astype(jnp.bfloat16)
        rows2[t * TILE : (t + 1) * TILE, :width] = low
        rows2[t * TILE : (t + 1) * TILE, width:] = low

    where_pair, where_panel = [], []
    for c in range(RADIX):
        low = c - pair_panel * pair_slots
        where_pair.append(jnp.where((low >= 0) & (low < pair_slots), low, junk))
        low = c - panel * panel_slots
        where_panel.append(jnp.where((low >= 0) & (low < panel_slots), low + pair_slots, junk))

    def forward(base, step):
        spectra[step % 2] = jnp.dot(
            rows2[pl.ds(base, TILE), :], table[step % n_groups], preferred_element_type=jnp.float32
        )

    def multiply(base, step):
        group = step % n_groups
        source = spectra.at[step % 2]
        target = products.at[step % 2]
        chunk = 32
        for r in range(0, TILE, chunk):
            third = cube[pl.ds(base + r, chunk), :]
            for side in range(2):
                a_re, a_im, b_re, b_im, c_re, c_im = [
                    source[r : r + chunk, i * WIDE + side * HALF : i * WIDE + (side + 1) * HALF]
                    for i in range(6)
                ]
                a_re, a_im = a_re * third, a_im * third
                if group == 0 and side == 0:
                    real = a_re * b_re
                    both = a_im * b_im
                    m_re, m_im = real - both, a_re * b_im + a_im * b_re
                    first = lax.broadcasted_iota(jnp.int32, real.shape, 1) == 0
                    out_re = jnp.where(first, real * c_re, m_re * c_re - m_im * c_im)
                    out_im = jnp.where(first, both * c_im, m_re * c_im + m_im * c_re)
                else:
                    m_re, m_im = a_re * b_re - a_im * b_im, a_re * b_im + a_im * b_re
                    out_re = m_re * c_re - m_im * c_im
                    out_im = m_re * c_im + m_im * c_re
                if group == 0:
                    re_at, im_at = 2 * side * HALF, (2 * side + 1) * HALF
                else:
                    re_at, im_at = side * HALF, WIDE + side * HALF
                target[r : r + chunk, re_at : re_at + HALF] = out_re.astype(jnp.bfloat16)
                target[r : r + chunk, im_at : im_at + HALF] = out_im.astype(jnp.bfloat16)

    def inverse(step):
        group = step % n_groups
        source = products.at[step % 2]
        into = sums[step // n_groups]
        if group == 0:
            for side in range(2):
                at = slice(side * WIDE, (side + 1) * WIDE)
                into[:, at] = jnp.dot(source[:, at], ends_table[:, at], preferred_element_type=jnp.float32)
        else:
            into[:, 2 * group * WIDE : 2 * (group + 1) * WIDE] = jnp.dot(
                source[...], groups_table[group - 1], preferred_element_type=jnp.float32
            )

    def finish(source, base, part, parts):
        chunk = 16
        size = TILE // parts
        for r in range(part * size, (part + 1) * size, chunk):
            for side in range(2):
                outs = combine(
                    lambda i: source[r : r + chunk, i * WIDE + side * HALF : i * WIDE + (side + 1) * HALF]
                )
                at = slice(side * HALF, (side + 1) * HALF)
                for c in range(RADIX):
                    value = outs[c].astype(jnp.bfloat16)
                    kept[where_pair[c], pl.ds(base + r, chunk), at] = value
                    kept[where_panel[c], pl.ds(base + r, chunk), at] = value

    steps = 2 * n_groups

    def pair_step(t, _):
        bases = [pl.multiple_of(2 * t * TILE, TILE), pl.multiple_of((2 * t + 1) * TILE, TILE)]
        before = [pl.multiple_of(jnp.maximum(2 * t - 1, 1) * TILE, TILE), bases[0]]
        forward(bases[0], 0)
        for step in range(steps):
            if step + 1 < steps:
                forward(bases[(step + 1) // n_groups], step + 1)
            multiply(bases[step // n_groups], step)
            inverse(step)
            which = step // n_groups
            finish(sums[1 - which], before[which], step % n_groups, n_groups)
        return 0

    lax.fori_loop(0, rows // (2 * TILE), pair_step, 0)
    for part in range(n_groups):
        finish(sums[1], rows - TILE, part, n_groups)

    odd = lax.rem(device, 2)
    each = pair_slots // 2
    for i in range(each):
        for who, target in ((1 - odd, send_ref), (odd, own_ref)):
            left = kept[who * each + i].T
            for j in range(panel_slots):
                target[i * WIDE : (i + 1) * WIDE, j * WIDE : (j + 1) * WIDE] = jnp.dot(
                    left, kept[pair_slots + j], preferred_element_type=jnp.float32
                ).astype(target.dtype)
    for j in range(panel_slots):
        line = jnp.dot(marks, kept[pair_slots + j], preferred_element_type=jnp.float32)
        at = slice(j * WIDE, (j + 1) * WIDE)
        own_ref[each * WIDE : each * WIDE + 8, at] = line
        send_ref[each * WIDE :, at] = jnp.concatenate([line, line], axis=0).astype(send_ref.dtype)


def body(samples, targets, counts, bucket_ids, sign_bits):
    n_dp, n_feat = lax.axis_size("dp"), lax.axis_size("feat")
    slots, width = samples.shape
    half = slots // 2
    total = half * n_dp
    rows = total // 2
    scalars = [pl.BlockSpec(memory_space=pltpu.SMEM)]
    vector = pl.BlockSpec(memory_space=pltpu.VMEM)

    message = jax.ShapeDtypeStruct((half + PAD + TAIL, width), jnp.bfloat16)
    own, other = pl.pallas_call(
        prepare_kernel,
        out_shape=(message, message),
        in_specs=scalars + [vector] * 2,
        out_specs=(vector, vector),
    )(counts, samples, targets.reshape(1, slots))

    def swap(block, bit):
        return lax.ppermute(block, "dp", [(i, i ^ bit) for i in range(n_dp)])

    blocks = [own, swap(other, 1)]
    for delta in range(2, n_dp):
        bits = [1 << i for i in range(1, n_dp.bit_length()) if delta >> i & 1]
        bit = bits[0] if delta % 2 else bits[-1]
        blocks.append(swap(blocks[delta ^ bit], bit))

    table = forward_tables(bucket_ids, sign_bits)
    ends_table, group_table = inverse_tables()
    ends_table, group_table = jnp.asarray(ends_table), jnp.asarray(group_table)
    own_columns, panel_columns = SK // n_dp, SK // n_feat
    kept_slots = 2 * own_columns // WIDE + panel_columns // WIDE + 1
    span = -(-(rows + half + 2 * PAD + 8) // 128) * 128
    mine, send = pl.pallas_call(
        main_kernel,
        out_shape=(
            jax.ShapeDtypeStruct((own_columns + 8, panel_columns), jnp.float32),
            jax.ShapeDtypeStruct((own_columns + 16, panel_columns), jnp.bfloat16),
        ),
        in_specs=scalars + [vector] * (n_dp + 3),
        out_specs=(vector, vector),
        scratch_shapes=[
            pltpu.SMEM((n_dp,), jnp.int32),
            pltpu.VMEM((span, width), jnp.float32),
            pltpu.VMEM((rows, 2 * width), jnp.bfloat16),
            pltpu.VMEM((rows, 128), jnp.float32),
            pltpu.VMEM((2, TILE, 6 * WIDE), jnp.float32),
            pltpu.VMEM((2, TILE, 2 * WIDE), jnp.bfloat16),
            pltpu.VMEM((TILE, SK), jnp.float32),
            pltpu.VMEM((TILE, SK), jnp.float32),
            pltpu.VMEM((kept_slots, rows, WIDE), jnp.bfloat16),
        ],
        compiler_params=pltpu.CompilerParams(vmem_limit_bytes=VMEM_BYTES),
        cost_estimate=pl.CostEstimate(flops=3 * 10**10, bytes_accessed=24 * 10**6, transcendentals=0),
    )(counts, *blocks, table, ends_table, group_table)
    theirs = swap(send, 1)
    gram = (mine[:own_columns] + theirs[:own_columns].astype(jnp.float32)) * (1.0 / total)
    zty = (mine[own_columns] + theirs[own_columns].astype(jnp.float32)) * total ** (-0.5)
    return gram, zty


def solution(mesh):
    placed = (P("dp", None), P("dp"), P(), P(), P())
    return jax.shard_map(
        body, mesh=mesh, in_specs=placed, out_specs=(P("dp", "feat"), P("feat")), check_vma=False
    )
```

```python
import functools
import math

import jax
import jax.numpy as jnp
import numpy as np
from jax import lax
from jax.experimental import pallas as pl
from jax.experimental.pallas import tpu as pltpu
from jax.sharding import PartitionSpec as P

SK = 4096
RADIX = 16
WIDE = SK // RADIX
HALF = WIDE // 2
TILE = 256
TAIL = 16
PAD = 16
LOW = jnp.float8_e5m2
VMEM_BYTES = 25 * 1024 * 1024


def short_dft():
    index = np.arange(WIDE)[:, None] * np.arange(HALF)[None, :] % WIDE
    angle = index * (2.0 * np.pi / WIDE)
    terms = []
    for table in (np.cos(angle), -np.sin(angle)):
        rest = table.astype(np.float32)
        for _ in range(3):
            part = rest.astype(jnp.bfloat16)
            terms.append(part)
            rest = rest - part.astype(np.float32)
    return np.concatenate(terms, axis=1)


def inverse_tables():
    scale = SK ** (-0.5)
    column = np.arange(WIDE)[None, :]

    def trig(freq):
        angle = (freq[:, None] * column % SK) * (2.0 * np.pi / SK)
        return 2.0 * scale * np.cos(angle), 2.0 * scale * np.sin(angle)

    narrow = np.arange(HALF)
    cos_a, sin_a = trig(RADIX * narrow)
    cos_b, sin_b = trig(RADIX // 2 + RADIX * narrow)
    imag_a = -sin_a
    cos_a[0] = scale
    imag_a[0] = scale * (1.0 - 2.0 * (np.arange(WIDE) % 2))
    ends = np.concatenate(
        [np.concatenate([cos_a, imag_a], axis=0), np.concatenate([cos_b, -sin_b], axis=0)], axis=1
    )
    groups = []
    for group in range(1, RADIX // 2):
        cosine, sine = trig(group + RADIX * np.arange(WIDE))
        groups.append(
            np.concatenate(
                [np.concatenate([cosine, sine], axis=1), np.concatenate([-sine, cosine], axis=1)],
                axis=0,
            )
        )
    return ends.astype(jnp.bfloat16), np.stack(groups).astype(jnp.bfloat16)


def table_kernel(bucket_ref, phase_ref, dft_ref, high_ref, low_ref, base_ref):
    group = pl.program_id(0)
    sketches, features_in = 3, bucket_ref.shape[0]

    @pl.when(group == 0)
    def _():
        lane = lax.broadcasted_iota(jnp.int32, (features_in, WIDE), 1)
        for k in range(sketches):
            chosen = jnp.where(bucket_ref[:, k : k + 1] == lane, 1.0, 0.0).astype(jnp.bfloat16)
            full = jnp.dot(chosen, dft_ref[...], preferred_element_type=jnp.float32)
            for part in range(2):
                at = 3 * part * HALF
                base_ref[2 * k + part] = (
                    full[:, at : at + HALF]
                    + full[:, at + HALF : at + 2 * HALF]
                    + full[:, at + 2 * HALF : at + 3 * HALF]
                )

    first_lane = (lax.broadcasted_iota(jnp.int32, (features_in, HALF), 1) == 0) & (group == 0)
    for k in range(sketches):
        base_re, base_im = base_ref[2 * k], base_ref[2 * k + 1]
        for side in range(2):
            at = 6 * side + 2 * k
            turn_re, turn_im = phase_ref[0, :, at : at + 1], phase_ref[0, :, at + 1 : at + 2]
            real = turn_re * base_re - turn_im * base_im
            imag = turn_re * base_im + turn_im * base_re
            if side == 0:
                imag = jnp.where(first_lane, phase_ref[0, :, 12 + k : 13 + k], imag)
            for part, values in enumerate((real, imag)):
                start = (2 * k + part) * WIDE + side * HALF
                high = values.astype(jnp.bfloat16)
                high_ref[0, :, start : start + HALF] = high
                low_ref[0, :, start : start + HALF] = (values - high.astype(jnp.float32)).astype(LOW)


def forward_tables(bucket_ids, sign_bits):
    groups = RADIX // 2
    features_in = bucket_ids.shape[1]
    first = np.arange(groups)
    second = np.where(first == 0, RADIX // 2, first + RADIX * HALF)
    offsets = jnp.asarray(np.stack([first, second], axis=1), jnp.int32)
    buckets = bucket_ids.T
    signs = (2 * sign_bits - 1).astype(jnp.float32).T
    turns = buckets[None, :, None, :] * offsets[:, None, :, None] % SK
    angles = turns.astype(jnp.float32) * (2.0 * math.pi / SK)
    phases = jnp.stack([signs[None, :, None] * jnp.cos(angles), -signs[None, :, None] * jnp.sin(angles)], -1)
    phases = phases.reshape(groups, features_in, 12)
    middle = signs * (1 - 2 * (buckets % 2)).astype(jnp.float32)
    phases = jnp.concatenate([phases, jnp.broadcast_to(middle[None], (groups, features_in, 3))], -1)
    short = jnp.pad(buckets % WIDE, ((0, 0), (0, 5)))
    dft = jnp.asarray(short_dft())
    return pl.pallas_call(
        table_kernel,
        grid=(groups,),
        out_shape=(
            jax.ShapeDtypeStruct((groups, features_in, 6 * WIDE), jnp.bfloat16),
            jax.ShapeDtypeStruct((groups, features_in, 6 * WIDE), LOW),
        ),
        in_specs=[
            pl.BlockSpec(short.shape, lambda g: (0, 0)),
            pl.BlockSpec((1, features_in, 15), lambda g: (g, 0, 0)),
            pl.BlockSpec(dft.shape, lambda g: (0, 0)),
        ],
        out_specs=(pl.BlockSpec((1, features_in, 6 * WIDE), lambda g: (g, 0, 0)),) * 2,
        scratch_shapes=[pltpu.VMEM((6, features_in, HALF), jnp.float32)],
        compiler_params=pltpu.CompilerParams(vmem_limit_bytes=VMEM_BYTES // 2),
        cost_estimate=pl.CostEstimate(flops=2 * 10**9, bytes_accessed=14 * 10**6, transcendentals=0),
    )(short, phases, dft)


def combine(load):
    root = math.sqrt(0.5)
    big, small = math.cos(math.pi / 8), math.sin(math.pi / 8)
    r4, i4 = load(8), load(9)
    q0, q8 = load(0), load(1)
    a, b = q0 + q8, q0 - q8
    quarter = (a + r4, b - i4, a - r4, b + i4)
    r2, i2, r6, i6 = load(4), load(5), load(12), load(13)
    u, v = r2 - r6, i2 + i6
    other = (r2 + r6, root * (u - v), i6 - i2, -root * (u + v))
    even = [quarter[c] + other[c] for c in range(4)] + [quarter[c] - other[c] for c in range(4)]
    r1, i1, r7, i7 = load(2), load(3), load(14), load(15)
    r3, i3, r5, i5 = load(6), load(7), load(10), load(11)
    p1, q1, t1, s1 = r1 + r7, r1 - r7, i1 - i7, i1 + i7
    p3, q3, t3, s3 = r3 + r5, r3 - r5, i3 - i5, i3 + i5
    w, y = root * (p1 - p3), root * (t1 + t3)
    a1, b1 = q1 * big + q3 * small, s1 * small + s3 * big
    c1, d1 = q1 * small - q3 * big, s1 * big - s3 * small
    odd = [p1 + p3, a1 - b1, w - y, c1 - d1, t3 - t1, -(c1 + d1), -(w + y), -(a1 + b1)]
    return [even[c] + odd[c] for c in range(8)] + [even[c] - odd[c] for c in range(8)]


def window_start(first, slots):
    window = slots // 2 + PAD
    return pl.multiple_of(jnp.minimum(first // PAD * PAD, slots - window), PAD)


def prepare_kernel(counts_ref, samples_ref, targets_ref, own_ref, other_ref):
    device = lax.axis_index("dp")
    core = lax.rem(device, 2)
    slots, width = samples_ref.shape
    window = slots // 2 + PAD
    start = jnp.int32(0)
    for j in range(counts_ref.shape[0]):
        start = start + jnp.where(j < device, counts_ref[j], 0)
    cut = (start + counts_ref[device] + 1) // 2 - (start + 1) // 2
    late = window_start(cut, slots)
    lines = [targets_ref[:, i * width : (i + 1) * width] for i in range(slots // width)]
    lines.append(jnp.zeros((TAIL - len(lines), width), jnp.bfloat16))
    tail = jnp.concatenate(lines, axis=0)
    for target, is_late in ((own_ref, core), (other_ref, 1 - core)):
        begin = pl.multiple_of(late * is_late, PAD)
        target[:window, :] = samples_ref[pl.ds(begin, window), :]
        target[window:, :] = tail


def gather_rows(device, counts_ref, ends_ref, blocks, slots, loose, width, with_marks):
    core = lax.rem(device, 2)
    window = slots // 2 + PAD
    span = loose.shape[0]
    lane = lax.broadcasted_iota(jnp.int32, (8, span), 1)
    marks = jnp.zeros((8, span), jnp.float32)
    total = jnp.int32(0)
    for j in range(counts_ref.shape[0]):
        total = total + counts_ref[j]
        ends_ref[j] = total
    at = jnp.int32(0)
    for delta, block_ref in blocks:
        source = lax.bitwise_xor(device, delta)
        end = ends_ref[source]
        start = end - counts_ref[source]
        cut = (end + 1) // 2 - (start + 1) // 2
        share = jnp.where(core == 0, cut, end // 2 - start // 2)
        first = cut * core
        skip = first - window_start(cut, slots) * core
        base = at - skip + PAD
        spill = lax.rem(base, 8)
        begin = pl.multiple_of(base - spill, 8)
        block = block_ref[:window, :].astype(jnp.float32)
        block = jnp.concatenate([block, jnp.zeros((8, width), jnp.float32)], axis=0)
        block = pltpu.roll(block, spill, 0)
        edge = PAD + 8
        keep = lax.broadcasted_iota(jnp.int32, (edge, width), 0) < spill + skip
        loose[pl.ds(begin, edge), :] = jnp.where(keep, loose[pl.ds(begin, edge), :], block[:edge])
        loose[pl.ds(begin + edge, window + 8 - edge), :] = block[edge:]
        here, at = at, at + share
        if not with_marks:
            continue
        tail = block_ref[window:, :].astype(jnp.float32)
        line = jnp.concatenate([tail[i : i + 1, :] for i in range(slots // width)], axis=1)
        line = jnp.concatenate([line, jnp.zeros((1, span - slots), jnp.float32)], axis=1)
        line = pltpu.roll(jnp.broadcast_to(line, (8, span)), lax.rem(here - first + span, span), 1)
        marks = jnp.where((lane >= here) & (lane < at), line, marks)
    return marks


def main_kernel(deltas, first, final, counts_ref, *refs):
    count = len(deltas)
    blocks = list(zip(deltas, refs[:count]))
    high_table, low_table, ends_table, groups_table = refs[count : count + 4]
    if final:
        early = refs[count + 4] if first else None
        refs = refs[count + (5 if first else 4) :]
        own_ref, send_ref, kept = refs[0], refs[1], refs[-1]
        ends_ref, loose, rows2, rows_low, cube, spectra, products, sums_a, sums_b = refs[2:-1]
    else:
        kept, ends_ref, loose, rows2, rows_low, cube, spectra, products, sums_a, sums_b = refs[count + 4 :]
    sums = (sums_a, sums_b)
    device, panel = lax.axis_index("dp"), lax.axis_index("feat")
    pair_panel = device // 2
    n_groups = RADIX // 2
    width = rows2.shape[1]
    slots = 2 * (blocks[0][1].shape[0] - TAIL - PAD)
    rows = rows2.shape[0]
    pair_slots = 2 * SK // WIDE // lax.axis_size("dp")
    panel_slots = SK // WIDE // lax.axis_size("feat")
    junk = pair_slots + panel_slots

    marks = gather_rows(device, counts_ref, ends_ref, blocks, slots, loose, width, final)
    for t in range(rows // TILE):
        values = loose[PAD + first + t * TILE : PAD + first + (t + 1) * TILE, :]
        mean = jnp.sum(values * values, axis=1, keepdims=True) * (1.0 / width)
        factor = lax.rsqrt(mean + 1e-06) * width ** (-0.5)
        cube[t * TILE : (t + 1) * TILE, :] = jnp.broadcast_to(factor * factor * factor, (TILE, 128))
        rows2[t * TILE : (t + 1) * TILE, :] = values.astype(jnp.bfloat16)
        rows_low[t * TILE : (t + 1) * TILE, :] = values.astype(LOW)

    where_pair, where_panel = [], []
    for c in range(RADIX):
        low = c - pair_panel * pair_slots
        where_pair.append(jnp.where((low >= 0) & (low < pair_slots), low, junk))
        low = c - panel * panel_slots
        where_panel.append(jnp.where((low >= 0) & (low < panel_slots), low + pair_slots, junk))

    def forward(base, step):
        group, here = step % n_groups, pl.ds(base, TILE)
        spectra[step % 2] = jnp.dot(
            rows2[here, :], high_table[group], preferred_element_type=jnp.float32
        ) + jnp.dot(rows_low[here, :], low_table[group], preferred_element_type=jnp.float32)

    def multiply(base, step):
        group = step % n_groups
        source = spectra.at[step % 2]
        target = products.at[step % 2]
        chunk = 32
        for r in range(0, TILE, chunk):
            third = cube[pl.ds(base + r, chunk), :]
            for side in range(2):
                a_re, a_im, b_re, b_im, c_re, c_im = [
                    source[r : r + chunk, i * WIDE + side * HALF : i * WIDE + (side + 1) * HALF]
                    for i in range(6)
                ]
                a_re, a_im = a_re * third, a_im * third
                if group == 0 and side == 0:
                    real = a_re * b_re
                    both = a_im * b_im
                    m_re, m_im = real - both, a_re * b_im + a_im * b_re
                    first = lax.broadcasted_iota(jnp.int32, real.shape, 1) == 0
                    out_re = jnp.where(first, real * c_re, m_re * c_re - m_im * c_im)
                    out_im = jnp.where(first, both * c_im, m_re * c_im + m_im * c_re)
                else:
                    m_re, m_im = a_re * b_re - a_im * b_im, a_re * b_im + a_im * b_re
                    out_re = m_re * c_re - m_im * c_im
                    out_im = m_re * c_im + m_im * c_re
                if group == 0:
                    re_at, im_at = 2 * side * HALF, (2 * side + 1) * HALF
                else:
                    re_at, im_at = side * HALF, WIDE + side * HALF
                target[r : r + chunk, re_at : re_at + HALF] = out_re.astype(jnp.bfloat16)
                target[r : r + chunk, im_at : im_at + HALF] = out_im.astype(jnp.bfloat16)

    def inverse(step):
        group = step % n_groups
        source = products.at[step % 2]
        into = sums[step // n_groups]
        if group == 0:
            for side in range(2):
                at = slice(side * WIDE, (side + 1) * WIDE)
                into[:, at] = jnp.dot(source[:, at], ends_table[:, at], preferred_element_type=jnp.float32)
        else:
            into[:, 2 * group * WIDE : 2 * (group + 1) * WIDE] = jnp.dot(
                source[...], groups_table[group - 1], preferred_element_type=jnp.float32
            )

    def finish(source, base, part, parts):
        chunk = 16
        size = TILE // parts
        for r in range(part * size, (part + 1) * size, chunk):
            for side in range(2):
                outs = combine(
                    lambda i: source[r : r + chunk, i * WIDE + side * HALF : i * WIDE + (side + 1) * HALF]
                )
                at = slice(side * HALF, (side + 1) * HALF)
                for c in range(RADIX):
                    value = outs[c].astype(jnp.bfloat16)
                    kept[where_pair[c], pl.ds(base + r, chunk), at] = value
                    kept[where_panel[c], pl.ds(base + r, chunk), at] = value

    steps = 2 * n_groups

    def pair_step(t, _):
        bases = [pl.multiple_of(2 * t * TILE, TILE), pl.multiple_of((2 * t + 1) * TILE, TILE)]
        before = [pl.multiple_of(jnp.maximum(2 * t - 1, 1) * TILE, TILE), bases[0]]
        forward(bases[0], 0)
        for step in range(steps):
            if step + 1 < steps:
                forward(bases[(step + 1) // n_groups], step + 1)
            multiply(bases[step // n_groups], step)
            inverse(step)
            which = step // n_groups
            finish(sums[1 - which], before[which], step % n_groups, n_groups)
        return 0

    lax.fori_loop(0, rows // (2 * TILE), pair_step, 0)
    for part in range(n_groups):
        finish(sums[1], rows - TILE, part, n_groups)

    if not final:
        return
    odd = lax.rem(device, 2)
    each = pair_slots // 2
    marks = marks[:, : first + rows].astype(jnp.bfloat16)
    for i in range(each):
        for who, target in ((1 - odd, send_ref), (odd, own_ref)):
            left = kept[who * each + i].T
            left_early = early[who * each + i].T if first else None
            for j in range(panel_slots):
                block = jnp.dot(left, kept[pair_slots + j], preferred_element_type=jnp.float32)
                if first:
                    block += jnp.dot(left_early, early[pair_slots + j], preferred_element_type=jnp.float32)
                target[i * WIDE : (i + 1) * WIDE, j * WIDE : (j + 1) * WIDE] = block.astype(target.dtype)
    for j in range(panel_slots):
        line = jnp.dot(marks[:, first:], kept[pair_slots + j], preferred_element_type=jnp.float32)
        if first:
            line += jnp.dot(marks[:, :first], early[pair_slots + j], preferred_element_type=jnp.float32)
        at = slice(j * WIDE, (j + 1) * WIDE)
        own_ref[each * WIDE : each * WIDE + 8, at] = line
        send_ref[each * WIDE :, at] = jnp.concatenate([line, line], axis=0).astype(send_ref.dtype)


def body(samples, targets, counts, bucket_ids, sign_bits):
    n_dp, n_feat = lax.axis_size("dp"), lax.axis_size("feat")
    slots, width = samples.shape
    half = slots // 2
    total = half * n_dp
    rows = total // 2
    scalars = [pl.BlockSpec(memory_space=pltpu.SMEM)]
    vector = pl.BlockSpec(memory_space=pltpu.VMEM)

    message = jax.ShapeDtypeStruct((half + PAD + TAIL, width), jnp.bfloat16)
    own, other = pl.pallas_call(
        prepare_kernel,
        out_shape=(message, message),
        in_specs=scalars + [vector] * 2,
        out_specs=(vector, vector),
    )(counts, samples, targets.reshape(1, slots))

    def swap(block, bit):
        return lax.ppermute(block, "dp", [(i, i ^ bit) for i in range(n_dp)])

    high_table, low_table = forward_tables(bucket_ids, sign_bits)
    blocks = {0: own, 1: swap(other, 1)}
    near = [0, 1]
    for i in range(1, (n_dp - 1).bit_length()):
        for core in range(2):
            blocks[(1 << i) + core] = swap(blocks[core], 1 << i)
            near.append((1 << i) + core)
    far = [delta for delta in range(n_dp) if delta not in blocks]
    sure = max(0, total - slots * len(far) - len(near)) // 2 if far else 0
    first = min(sure, rows // 3) // (2 * TILE) * 2 * TILE
    if first:
        high_table, sources = lax.optimization_barrier((high_table, dict(blocks)))
        blocks.update(sources)
    for delta in far:
        bits = [1 << i for i in range(1, n_dp.bit_length()) if delta >> i & 1]
        bit = bits[0] if delta % 2 else bits[-1]
        blocks[delta] = swap(blocks[delta ^ bit], bit)

    ends_table, group_table = inverse_tables()
    tables = (high_table, low_table, jnp.asarray(ends_table), jnp.asarray(group_table))
    own_columns, panel_columns = SK // n_dp, SK // n_feat
    kept_slots = 2 * own_columns // WIDE + panel_columns // WIDE + 1
    span = -(-(rows + half + 2 * PAD + 8) // 128) * 128

    def transform(deltas, begin, end, final, more):
        size = end - begin
        kept = (kept_slots, size, WIDE)
        out_shape = jax.ShapeDtypeStruct(kept, jnp.bfloat16)
        if final:
            out_shape = (
                jax.ShapeDtypeStruct((own_columns + 8, panel_columns), jnp.float32),
                jax.ShapeDtypeStruct((own_columns + 16, panel_columns), jnp.bfloat16),
            )
        scratch = [
            pltpu.SMEM((n_dp,), jnp.int32),
            pltpu.VMEM((span, width), jnp.float32),
            pltpu.VMEM((size, width), jnp.bfloat16),
            pltpu.VMEM((size, width), LOW),
            pltpu.VMEM((size, 128), jnp.float32),
            pltpu.VMEM((2, TILE, 6 * WIDE), jnp.float32),
            pltpu.VMEM((2, TILE, 2 * WIDE), jnp.bfloat16),
            pltpu.VMEM((TILE, SK), jnp.float32),
            pltpu.VMEM((TILE, SK), jnp.float32),
        ]
        return pl.pallas_call(
            functools.partial(main_kernel, deltas, begin, final),
            out_shape=out_shape,
            in_specs=scalars + [vector] * (len(deltas) + 4 + len(more)),
            out_specs=(vector, vector) if final else vector,
            scratch_shapes=scratch + ([pltpu.VMEM(kept, jnp.bfloat16)] if final else []),
            compiler_params=pltpu.CompilerParams(vmem_limit_bytes=VMEM_BYTES),
            cost_estimate=pl.CostEstimate(
                flops=2 * 10**7 * size, bytes_accessed=24 * 10**6, transcendentals=0
            ),
        )(counts, *[blocks[delta] for delta in deltas], *tables, *more)

    early = (transform(near, 0, first, False, ()),) if first else ()
    mine, send = transform(near + far, first, rows, True, early)
    theirs = swap(send, 1)
    gram = (mine[:own_columns] + theirs[:own_columns].astype(jnp.float32)) * (1.0 / total)
    zty = (mine[own_columns] + theirs[own_columns].astype(jnp.float32)) * total ** (-0.5)
    return gram, zty


def solution(mesh):
    placed = (P("dp", None), P("dp"), P(), P(), P())
    return jax.shard_map(
        body, mesh=mesh, in_specs=placed, out_specs=(P("dp", "feat"), P("feat")), check_vma=False
    )
```

```python
import functools
import math

import jax
import jax.numpy as jnp
import numpy as np
from jax import lax
from jax.experimental import pallas as pl
from jax.experimental.pallas import tpu as pltpu
from jax.sharding import PartitionSpec as P

SK = 4096
RADIX = 16
WIDE = SK // RADIX
HALF = WIDE // 2
TILE = 256
TAIL = 16
PAD = 16
LOW = jnp.float8_e5m2
VMEM_BYTES = 25 * 1024 * 1024


def three_terms(tables):
    terms = []
    for table in tables:
        rest = table.astype(np.float32)
        for _ in range(3):
            part = rest.astype(jnp.bfloat16)
            terms.append(part)
            rest = rest - part.astype(np.float32)
    return np.concatenate(terms, axis=1)


def turn_tables():
    groups = RADIX // 2
    first = np.arange(groups)
    second = np.where(first == 0, RADIX // 2, first + RADIX * HALF)
    starts = np.zeros(HALF, np.int64)
    starts[: 2 * groups] = np.concatenate([first, second])
    low, high = np.arange(WIDE)[:, None], np.arange(HALF)[:, None]
    angles = [
        low * np.arange(HALF)[None, :] % WIDE * (2.0 * np.pi / WIDE),
        low * starts[None, :] % SK * (2.0 * np.pi / SK),
        high * starts[None, :] % RADIX * (2.0 * np.pi / RADIX),
    ]
    pairs = [three_terms([np.cos(angle), -np.sin(angle)]) for angle in angles]
    return np.concatenate(pairs[:2], axis=1), pairs[2]


def inverse_tables():
    scale = SK ** (-0.5)
    column = np.arange(WIDE)[None, :]

    def trig(freq):
        angle = (freq[:, None] * column % SK) * (2.0 * np.pi / SK)
        return 2.0 * scale * np.cos(angle), 2.0 * scale * np.sin(angle)

    narrow = np.arange(HALF)
    cos_a, sin_a = trig(RADIX * narrow)
    cos_b, sin_b = trig(RADIX // 2 + RADIX * narrow)
    imag_a = -sin_a
    cos_a[0] = scale
    imag_a[0] = scale * (1.0 - 2.0 * (np.arange(WIDE) % 2))
    ends = np.concatenate(
        [np.concatenate([cos_a, imag_a], axis=0), np.concatenate([cos_b, -sin_b], axis=0)], axis=1
    )
    groups = []
    for group in range(1, RADIX // 2):
        cosine, sine = trig(group + RADIX * np.arange(WIDE))
        groups.append(
            np.concatenate(
                [np.concatenate([cosine, sine], axis=1), np.concatenate([-sine, cosine], axis=1)],
                axis=0,
            )
        )
    return ends.astype(jnp.bfloat16), np.stack(groups).astype(jnp.bfloat16)


def table_kernel(bucket_ref, sign_ref, low_turns_ref, high_turns_ref, high_ref, low_ref):
    sketches, features_in = bucket_ref.shape
    groups = RADIX // 2
    blank = jnp.zeros((8 - 2 * sketches, features_in), jnp.float32)
    columns = jnp.concatenate(
        [bucket_ref[...].astype(jnp.float32), sign_ref[...].astype(jnp.float32), blank], axis=0
    ).T

    def three(full, at):
        return full[:, at : at + HALF] + full[:, at + HALF : at + 2 * HALF] + full[:, at + 2 * HALF : at + 3 * HALF]

    chunk = 64
    for k in range(sketches):
        bucket = columns[:, k : k + 1].astype(jnp.int32)
        sign = 2.0 * columns[:, sketches + k : sketches + k + 1] - 1.0
        lane = lax.broadcasted_iota(jnp.int32, (features_in, WIDE), 1)
        chosen = jnp.where(bucket % WIDE == lane, 1.0, 0.0).astype(jnp.bfloat16)
        full = jnp.dot(chosen, low_turns_ref[...], preferred_element_type=jnp.float32)
        base_re, base_im, fine_re, fine_im = [three(full, 3 * i * HALF) for i in range(4)]
        lane = lax.broadcasted_iota(jnp.int32, (features_in, HALF), 1)
        chosen = jnp.where(bucket // WIDE == lane, 1.0, 0.0).astype(jnp.bfloat16)
        full = jnp.dot(chosen, high_turns_ref[...], preferred_element_type=jnp.float32)
        wide_re, wide_im = three(full, 0), three(full, 3 * HALF)
        turns_re = (fine_re * wide_re - fine_im * wide_im) * sign
        turns_im = (fine_re * wide_im + fine_im * wide_re) * sign
        middle = sign * (1 - 2 * (bucket % 2)).astype(jnp.float32)
        for r in range(0, features_in, chunk):
            rows = slice(r, r + chunk)
            first_lane = lax.broadcasted_iota(jnp.int32, (chunk, HALF), 1) == 0
            for group in range(groups):
                for side in range(2):
                    at = side * groups + group
                    turn_re, turn_im = turns_re[rows, at : at + 1], turns_im[rows, at : at + 1]
                    real = turn_re * base_re[rows] - turn_im * base_im[rows]
                    imag = turn_re * base_im[rows] + turn_im * base_re[rows]
                    if group == 0 and side == 0:
                        imag = jnp.where(first_lane, middle[rows], imag)
                    for part, values in enumerate((real, imag)):
                        start = (2 * k + part) * WIDE + side * HALF
                        high = values.astype(jnp.bfloat16)
                        high_ref[group, rows, start : start + HALF] = high
                        low_ref[group, rows, start : start + HALF] = (
                            values - high.astype(jnp.float32)
                        ).astype(LOW)


def forward_tables(bucket_ids, sign_bits):
    shape = (RADIX // 2, bucket_ids.shape[1], 6 * WIDE)
    low_turns, high_turns = turn_tables()
    vector = pl.BlockSpec(memory_space=pltpu.VMEM)
    return pl.pallas_call(
        table_kernel,
        out_shape=(jax.ShapeDtypeStruct(shape, jnp.bfloat16), jax.ShapeDtypeStruct(shape, LOW)),
        in_specs=[vector] * 4,
        out_specs=(vector, vector),
        compiler_params=pltpu.CompilerParams(vmem_limit_bytes=VMEM_BYTES // 2),
        cost_estimate=pl.CostEstimate(flops=2 * 10**9, bytes_accessed=14 * 10**6, transcendentals=0),
    )(bucket_ids, sign_bits, jnp.asarray(low_turns), jnp.asarray(high_turns))


def combine(load):
    root = math.sqrt(0.5)
    big, small = math.cos(math.pi / 8), math.sin(math.pi / 8)
    r4, i4 = load(8), load(9)
    q0, q8 = load(0), load(1)
    a, b = q0 + q8, q0 - q8
    quarter = (a + r4, b - i4, a - r4, b + i4)
    r2, i2, r6, i6 = load(4), load(5), load(12), load(13)
    u, v = r2 - r6, i2 + i6
    other = (r2 + r6, root * (u - v), i6 - i2, -root * (u + v))
    even = [quarter[c] + other[c] for c in range(4)] + [quarter[c] - other[c] for c in range(4)]
    r1, i1, r7, i7 = load(2), load(3), load(14), load(15)
    r3, i3, r5, i5 = load(6), load(7), load(10), load(11)
    p1, q1, t1, s1 = r1 + r7, r1 - r7, i1 - i7, i1 + i7
    p3, q3, t3, s3 = r3 + r5, r3 - r5, i3 - i5, i3 + i5
    w, y = root * (p1 - p3), root * (t1 + t3)
    a1, b1 = q1 * big + q3 * small, s1 * small + s3 * big
    c1, d1 = q1 * small - q3 * big, s1 * big - s3 * small
    odd = [p1 + p3, a1 - b1, w - y, c1 - d1, t3 - t1, -(c1 + d1), -(w + y), -(a1 + b1)]
    return [even[c] + odd[c] for c in range(8)] + [even[c] - odd[c] for c in range(8)]


def window_start(first, slots):
    window = slots // 2 + PAD
    return pl.multiple_of(jnp.minimum(first // PAD * PAD, slots - window), PAD)


def prepare_kernel(counts_ref, samples_ref, targets_ref, own_ref, other_ref):
    device = lax.axis_index("dp")
    core = lax.rem(device, 2)
    slots, width = samples_ref.shape
    window = slots // 2 + PAD
    start = jnp.int32(0)
    for j in range(counts_ref.shape[0]):
        start = start + jnp.where(j < device, counts_ref[j], 0)
    cut = (start + counts_ref[device] + 1) // 2 - (start + 1) // 2
    late = window_start(cut, slots)
    lines = [targets_ref[:, i * width : (i + 1) * width] for i in range(slots // width)]
    lines.append(jnp.zeros((TAIL - len(lines), width), jnp.bfloat16))
    tail = jnp.concatenate(lines, axis=0)
    for target, is_late in ((own_ref, core), (other_ref, 1 - core)):
        begin = pl.multiple_of(late * is_late, PAD)
        target[:window, :] = samples_ref[pl.ds(begin, window), :]
        target[window:, :] = tail


def gather_rows(device, counts_ref, ends_ref, blocks, slots, loose, width, with_marks):
    core = lax.rem(device, 2)
    window = slots // 2 + PAD
    span = loose.shape[0]
    lane = lax.broadcasted_iota(jnp.int32, (8, span), 1)
    marks = jnp.zeros((8, span), jnp.float32)
    total = jnp.int32(0)
    for j in range(counts_ref.shape[0]):
        total = total + counts_ref[j]
        ends_ref[j] = total
    at = jnp.int32(0)
    for delta, block_ref in blocks:
        source = lax.bitwise_xor(device, delta)
        end = ends_ref[source]
        start = end - counts_ref[source]
        cut = (end + 1) // 2 - (start + 1) // 2
        share = jnp.where(core == 0, cut, end // 2 - start // 2)
        first = cut * core
        skip = first - window_start(cut, slots) * core
        base = at - skip + PAD
        spill = lax.rem(base, 8)
        begin = pl.multiple_of(base - spill, 8)
        block = block_ref[:window, :].astype(jnp.float32)
        block = jnp.concatenate([block, jnp.zeros((8, width), jnp.float32)], axis=0)
        block = pltpu.roll(block, spill, 0)
        edge = PAD + 8
        keep = lax.broadcasted_iota(jnp.int32, (edge, width), 0) < spill + skip
        loose[pl.ds(begin, edge), :] = jnp.where(keep, loose[pl.ds(begin, edge), :], block[:edge])
        loose[pl.ds(begin + edge, window + 8 - edge), :] = block[edge:]
        here, at = at, at + share
        if not with_marks:
            continue
        tail = block_ref[window:, :].astype(jnp.float32)
        line = jnp.concatenate([tail[i : i + 1, :] for i in range(slots // width)], axis=1)
        line = jnp.concatenate([line, jnp.zeros((1, span - slots), jnp.float32)], axis=1)
        line = pltpu.roll(jnp.broadcast_to(line, (8, span)), lax.rem(here - first + span, span), 1)
        marks = jnp.where((lane >= here) & (lane < at), line, marks)
    return marks


def main_kernel(deltas, first, final, counts_ref, *refs):
    count = len(deltas)
    blocks = list(zip(deltas, refs[:count]))
    high_table, low_table, ends_table, groups_table = refs[count : count + 4]
    if final:
        early = refs[count + 4] if first else None
        refs = refs[count + (5 if first else 4) :]
        own_ref, send_ref, kept = refs[0], refs[1], refs[-1]
        ends_ref, loose, rows2, rows_low, cube, spectra, products, sums_a, sums_b = refs[2:-1]
    else:
        kept, ends_ref, loose, rows2, rows_low, cube, spectra, products, sums_a, sums_b = refs[count + 4 :]
    sums = (sums_a, sums_b)
    device, panel = lax.axis_index("dp"), lax.axis_index("feat")
    pair_panel = device // 2
    n_groups = RADIX // 2
    width = rows2.shape[1]
    slots = 2 * (blocks[0][1].shape[0] - TAIL - PAD)
    rows = rows2.shape[0]
    pair_slots = 2 * SK // WIDE // lax.axis_size("dp")
    panel_slots = SK // WIDE // lax.axis_size("feat")
    junk = pair_slots + panel_slots

    marks = gather_rows(device, counts_ref, ends_ref, blocks, slots, loose, width, final)
    for t in range(rows // TILE):
        values = loose[PAD + first + t * TILE : PAD + first + (t + 1) * TILE, :]
        mean = jnp.sum(values * values, axis=1, keepdims=True) * (1.0 / width)
        factor = lax.rsqrt(mean + 1e-06) * width ** (-0.5)
        cube[t * TILE : (t + 1) * TILE, :] = jnp.broadcast_to(factor * factor * factor, (TILE, 128))
        rows2[t * TILE : (t + 1) * TILE, :] = values.astype(jnp.bfloat16)
        rows_low[t * TILE : (t + 1) * TILE, :] = values.astype(LOW)

    where_pair, where_panel = [], []
    for c in range(RADIX):
        low = c - pair_panel * pair_slots
        where_pair.append(jnp.where((low >= 0) & (low < pair_slots), low, junk))
        low = c - panel * panel_slots
        where_panel.append(jnp.where((low >= 0) & (low < panel_slots), low + pair_slots, junk))

    def forward(base, step):
        group, here = step % n_groups, pl.ds(base, TILE)
        spectra[step % 2] = jnp.dot(
            rows2[here, :], high_table[group], preferred_element_type=jnp.float32
        ) + jnp.dot(rows_low[here, :], low_table[group], preferred_element_type=jnp.float32)

    def multiply(base, step):
        group = step % n_groups
        source = spectra.at[step % 2]
        target = products.at[step % 2]
        chunk = 32
        for r in range(0, TILE, chunk):
            third = cube[pl.ds(base + r, chunk), :]
            for side in range(2):
                a_re, a_im, b_re, b_im, c_re, c_im = [
                    source[r : r + chunk, i * WIDE + side * HALF : i * WIDE + (side + 1) * HALF]
                    for i in range(6)
                ]
                a_re, a_im = a_re * third, a_im * third
                if group == 0 and side == 0:
                    real = a_re * b_re
                    both = a_im * b_im
                    m_re, m_im = real - both, a_re * b_im + a_im * b_re
                    first = lax.broadcasted_iota(jnp.int32, real.shape, 1) == 0
                    out_re = jnp.where(first, real * c_re, m_re * c_re - m_im * c_im)
                    out_im = jnp.where(first, both * c_im, m_re * c_im + m_im * c_re)
                else:
                    m_re, m_im = a_re * b_re - a_im * b_im, a_re * b_im + a_im * b_re
                    out_re = m_re * c_re - m_im * c_im
                    out_im = m_re * c_im + m_im * c_re
                if group == 0:
                    re_at, im_at = 2 * side * HALF, (2 * side + 1) * HALF
                else:
                    re_at, im_at = side * HALF, WIDE + side * HALF
                target[r : r + chunk, re_at : re_at + HALF] = out_re.astype(jnp.bfloat16)
                target[r : r + chunk, im_at : im_at + HALF] = out_im.astype(jnp.bfloat16)

    def inverse(step):
        group = step % n_groups
        source = products.at[step % 2]
        into = sums[step // n_groups]
        if group == 0:
            for side in range(2):
                at = slice(side * WIDE, (side + 1) * WIDE)
                into[:, at] = jnp.dot(source[:, at], ends_table[:, at], preferred_element_type=jnp.float32)
        else:
            into[:, 2 * group * WIDE : 2 * (group + 1) * WIDE] = jnp.dot(
                source[...], groups_table[group - 1], preferred_element_type=jnp.float32
            )

    def finish(source, base, part, parts):
        chunk = 16
        size = TILE // parts
        for r in range(part * size, (part + 1) * size, chunk):
            for side in range(2):
                outs = combine(
                    lambda i: source[r : r + chunk, i * WIDE + side * HALF : i * WIDE + (side + 1) * HALF]
                )
                at = slice(side * HALF, (side + 1) * HALF)
                for c in range(RADIX):
                    value = outs[c].astype(jnp.bfloat16)
                    kept[where_pair[c], pl.ds(base + r, chunk), at] = value
                    kept[where_panel[c], pl.ds(base + r, chunk), at] = value

    steps = 2 * n_groups

    def pair_step(t, _):
        bases = [pl.multiple_of(2 * t * TILE, TILE), pl.multiple_of((2 * t + 1) * TILE, TILE)]
        before = [pl.multiple_of(jnp.maximum(2 * t - 1, 1) * TILE, TILE), bases[0]]
        forward(bases[0], 0)
        for step in range(steps):
            if step + 1 < steps:
                forward(bases[(step + 1) // n_groups], step + 1)
            multiply(bases[step // n_groups], step)
            inverse(step)
            which = step // n_groups
            finish(sums[1 - which], before[which], step % n_groups, n_groups)
        return 0

    lax.fori_loop(0, rows // (2 * TILE), pair_step, 0)
    for part in range(n_groups):
        finish(sums[1], rows - TILE, part, n_groups)

    if not final:
        return
    odd = lax.rem(device, 2)
    each = pair_slots // 2
    marks = marks[:, : first + rows].astype(jnp.bfloat16)
    for i in range(each):
        for who, target in ((1 - odd, send_ref), (odd, own_ref)):
            left = kept[who * each + i].T
            left_early = early[who * each + i].T if first else None
            for j in range(panel_slots):
                block = jnp.dot(left, kept[pair_slots + j], preferred_element_type=jnp.float32)
                if first:
                    block += jnp.dot(left_early, early[pair_slots + j], preferred_element_type=jnp.float32)
                target[i * WIDE : (i + 1) * WIDE, j * WIDE : (j + 1) * WIDE] = block.astype(target.dtype)
    for j in range(panel_slots):
        line = jnp.dot(marks[:, first:], kept[pair_slots + j], preferred_element_type=jnp.float32)
        if first:
            line += jnp.dot(marks[:, :first], early[pair_slots + j], preferred_element_type=jnp.float32)
        at = slice(j * WIDE, (j + 1) * WIDE)
        own_ref[each * WIDE : each * WIDE + 8, at] = line
        send_ref[each * WIDE :, at] = jnp.concatenate([line, line], axis=0).astype(send_ref.dtype)


def body(samples, targets, counts, bucket_ids, sign_bits):
    n_dp, n_feat = lax.axis_size("dp"), lax.axis_size("feat")
    slots, width = samples.shape
    half = slots // 2
    total = half * n_dp
    rows = total // 2
    scalars = [pl.BlockSpec(memory_space=pltpu.SMEM)]
    vector = pl.BlockSpec(memory_space=pltpu.VMEM)

    message = jax.ShapeDtypeStruct((half + PAD + TAIL, width), jnp.bfloat16)
    own, other = pl.pallas_call(
        prepare_kernel,
        out_shape=(message, message),
        in_specs=scalars + [vector] * 2,
        out_specs=(vector, vector),
    )(counts, samples, targets.reshape(1, slots))

    def swap(block, bit):
        return lax.ppermute(block, "dp", [(i, i ^ bit) for i in range(n_dp)])

    high_table, low_table = forward_tables(bucket_ids, sign_bits)
    blocks = {0: own, 1: swap(other, 1)}
    near = [0, 1]
    for i in range(1, (n_dp - 1).bit_length()):
        for core in range(2):
            blocks[(1 << i) + core] = swap(other if core else own, (1 << i) + core)
            near.append((1 << i) + core)
    far = [delta for delta in range(n_dp) if delta not in blocks]
    sure = max(0, total - slots * len(far) - len(near)) // 2 if far else 0
    first = min(sure, rows // 3) // (2 * TILE) * 2 * TILE
    if first:
        high_table, sources = lax.optimization_barrier((high_table, dict(blocks)))
        blocks.update(sources)
    for delta in far:
        bits = [1 << i for i in range(1, n_dp.bit_length()) if delta >> i & 1]
        bit = bits[0] if delta % 2 else bits[-1]
        blocks[delta] = swap(blocks[delta ^ bit], bit)

    ends_table, group_table = inverse_tables()
    tables = (high_table, low_table, jnp.asarray(ends_table), jnp.asarray(group_table))
    own_columns, panel_columns = SK // n_dp, SK // n_feat
    kept_slots = 2 * own_columns // WIDE + panel_columns // WIDE + 1
    span = -(-(rows + half + 2 * PAD + 8) // 128) * 128

    def transform(deltas, begin, end, final, more):
        size = end - begin
        kept = (kept_slots, size, WIDE)
        out_shape = jax.ShapeDtypeStruct(kept, jnp.bfloat16)
        if final:
            out_shape = (
                jax.ShapeDtypeStruct((own_columns + 8, panel_columns), jnp.float32),
                jax.ShapeDtypeStruct((own_columns + 16, panel_columns), jnp.bfloat16),
            )
        scratch = [
            pltpu.SMEM((n_dp,), jnp.int32),
            pltpu.VMEM((span, width), jnp.float32),
            pltpu.VMEM((size, width), jnp.bfloat16),
            pltpu.VMEM((size, width), LOW),
            pltpu.VMEM((size, 128), jnp.float32),
            pltpu.VMEM((2, TILE, 6 * WIDE), jnp.float32),
            pltpu.VMEM((2, TILE, 2 * WIDE), jnp.bfloat16),
            pltpu.VMEM((TILE, SK), jnp.float32),
            pltpu.VMEM((TILE, SK), jnp.float32),
        ]
        return pl.pallas_call(
            functools.partial(main_kernel, deltas, begin, final),
            out_shape=out_shape,
            in_specs=scalars + [vector] * (len(deltas) + 4 + len(more)),
            out_specs=(vector, vector) if final else vector,
            scratch_shapes=scratch + ([pltpu.VMEM(kept, jnp.bfloat16)] if final else []),
            compiler_params=pltpu.CompilerParams(vmem_limit_bytes=VMEM_BYTES),
            cost_estimate=pl.CostEstimate(
                flops=2 * 10**7 * size, bytes_accessed=24 * 10**6, transcendentals=0
            ),
        )(counts, *[blocks[delta] for delta in deltas], *tables, *more)

    early = (transform(near, 0, first, False, ()),) if first else ()
    mine, send = transform(near + far, first, rows, True, early)
    theirs = swap(send, 1)
    gram = (mine[:own_columns] + theirs[:own_columns].astype(jnp.float32)) * (1.0 / total)
    zty = (mine[own_columns] + theirs[own_columns].astype(jnp.float32)) * total ** (-0.5)
    return gram, zty


def solution(mesh):
    placed = (P("dp", None), P("dp"), P(), P(), P())
    return jax.shard_map(
        body, mesh=mesh, in_specs=placed, out_specs=(P("dp", "feat"), P("feat")), check_vma=False
    )
```

```python
import functools
import math

import jax
import jax.numpy as jnp
import numpy as np
from jax import lax
from jax.experimental import pallas as pl
from jax.experimental.pallas import tpu as pltpu
from jax.sharding import PartitionSpec as P

SK = 4096
RADIX = 16
WIDE = SK // RADIX
HALF = WIDE // 2
TILE = 256
TAIL = 16
PAD = 16
LOW = jnp.float8_e5m2
VMEM_BYTES = 25 * 1024 * 1024


def three_terms(tables):
    terms = []
    for table in tables:
        rest = table.astype(np.float32)
        for _ in range(3):
            part = rest.astype(jnp.bfloat16)
            terms.append(part)
            rest = rest - part.astype(np.float32)
    return np.concatenate(terms, axis=1)


def turn_tables():
    groups = RADIX // 2
    first = np.arange(groups)
    second = np.where(first == 0, RADIX // 2, first + RADIX * HALF)
    starts = np.zeros(HALF, np.int64)
    starts[: 2 * groups] = np.concatenate([first, second])
    low, high = np.arange(WIDE)[:, None], np.arange(HALF)[:, None]
    angles = [
        low * np.arange(HALF)[None, :] % WIDE * (2.0 * np.pi / WIDE),
        low * starts[None, :] % SK * (2.0 * np.pi / SK),
        high * starts[None, :] % RADIX * (2.0 * np.pi / RADIX),
    ]
    pairs = [three_terms([np.cos(angle), -np.sin(angle)]) for angle in angles]
    return np.concatenate(pairs[:2], axis=1), pairs[2]


def inverse_tables():
    scale = SK ** (-0.5)
    column = np.arange(WIDE)[None, :]

    def trig(freq):
        angle = (freq[:, None] * column % SK) * (2.0 * np.pi / SK)
        return 2.0 * scale * np.cos(angle), 2.0 * scale * np.sin(angle)

    narrow = np.arange(HALF)
    cos_a, sin_a = trig(RADIX * narrow)
    cos_b, sin_b = trig(RADIX // 2 + RADIX * narrow)
    imag_a = -sin_a
    cos_a[0] = scale
    imag_a[0] = scale * (1.0 - 2.0 * (np.arange(WIDE) % 2))
    ends = np.concatenate(
        [np.concatenate([cos_a, imag_a], axis=0), np.concatenate([cos_b, -sin_b], axis=0)], axis=1
    )
    groups = []
    for group in range(1, RADIX // 2):
        cosine, sine = trig(group + RADIX * np.arange(WIDE))
        groups.append(
            np.concatenate(
                [np.concatenate([cosine, sine], axis=1), np.concatenate([-sine, cosine], axis=1)],
                axis=0,
            )
        )
    return ends.astype(jnp.bfloat16), np.stack(groups).astype(jnp.bfloat16)


def table_kernel(bucket_ref, sign_ref, low_turns_ref, high_turns_ref, high_ref, low_ref):
    sketches, features_in = bucket_ref.shape
    groups = RADIX // 2
    blank = jnp.zeros((8 - 2 * sketches, features_in), jnp.float32)
    columns = jnp.concatenate(
        [bucket_ref[...].astype(jnp.float32), sign_ref[...].astype(jnp.float32), blank], axis=0
    ).T

    def three(full, at):
        return full[:, at : at + HALF] + full[:, at + HALF : at + 2 * HALF] + full[:, at + 2 * HALF : at + 3 * HALF]

    chunk = 64
    for k in range(sketches):
        bucket = columns[:, k : k + 1].astype(jnp.int32)
        sign = 2.0 * columns[:, sketches + k : sketches + k + 1] - 1.0
        lane = lax.broadcasted_iota(jnp.int32, (features_in, WIDE), 1)
        chosen = jnp.where(bucket % WIDE == lane, 1.0, 0.0).astype(jnp.bfloat16)
        full = jnp.dot(chosen, low_turns_ref[...], preferred_element_type=jnp.float32)
        base_re, base_im, fine_re, fine_im = [three(full, 3 * i * HALF) for i in range(4)]
        lane = lax.broadcasted_iota(jnp.int32, (features_in, HALF), 1)
        chosen = jnp.where(bucket // WIDE == lane, 1.0, 0.0).astype(jnp.bfloat16)
        full = jnp.dot(chosen, high_turns_ref[...], preferred_element_type=jnp.float32)
        wide_re, wide_im = three(full, 0), three(full, 3 * HALF)
        turns_re = (fine_re * wide_re - fine_im * wide_im) * sign
        turns_im = (fine_re * wide_im + fine_im * wide_re) * sign
        middle = sign * (1 - 2 * (bucket % 2)).astype(jnp.float32)
        for r in range(0, features_in, chunk):
            rows = slice(r, r + chunk)
            first_lane = lax.broadcasted_iota(jnp.int32, (chunk, HALF), 1) == 0
            for group in range(groups):
                for side in range(2):
                    at = side * groups + group
                    turn_re, turn_im = turns_re[rows, at : at + 1], turns_im[rows, at : at + 1]
                    real = turn_re * base_re[rows] - turn_im * base_im[rows]
                    imag = turn_re * base_im[rows] + turn_im * base_re[rows]
                    if group == 0 and side == 0:
                        imag = jnp.where(first_lane, middle[rows], imag)
                    for part, values in enumerate((real, imag)):
                        start = (2 * k + part) * WIDE + side * HALF
                        high = values.astype(jnp.bfloat16)
                        high_ref[group, rows, start : start + HALF] = high
                        low_ref[group, rows, start : start + HALF] = (
                            values - high.astype(jnp.float32)
                        ).astype(LOW)


def forward_tables(bucket_ids, sign_bits):
    shape = (RADIX // 2, bucket_ids.shape[1], 6 * WIDE)
    low_turns, high_turns = turn_tables()
    vector = pl.BlockSpec(memory_space=pltpu.VMEM)
    return pl.pallas_call(
        table_kernel,
        out_shape=(jax.ShapeDtypeStruct(shape, jnp.bfloat16), jax.ShapeDtypeStruct(shape, LOW)),
        in_specs=[vector] * 4,
        out_specs=(vector, vector),
        compiler_params=pltpu.CompilerParams(vmem_limit_bytes=VMEM_BYTES // 2),
        cost_estimate=pl.CostEstimate(flops=2 * 10**9, bytes_accessed=14 * 10**6, transcendentals=0),
    )(bucket_ids, sign_bits, jnp.asarray(low_turns), jnp.asarray(high_turns))


def combine(load):
    root = math.sqrt(0.5)
    big, small = math.cos(math.pi / 8), math.sin(math.pi / 8)
    r4, i4 = load(8), load(9)
    q0, q8 = load(0), load(1)
    a, b = q0 + q8, q0 - q8
    quarter = (a + r4, b - i4, a - r4, b + i4)
    r2, i2, r6, i6 = load(4), load(5), load(12), load(13)
    u, v = r2 - r6, i2 + i6
    other = (r2 + r6, root * (u - v), i6 - i2, -root * (u + v))
    even = [quarter[c] + other[c] for c in range(4)] + [quarter[c] - other[c] for c in range(4)]
    r1, i1, r7, i7 = load(2), load(3), load(14), load(15)
    r3, i3, r5, i5 = load(6), load(7), load(10), load(11)
    p1, q1, t1, s1 = r1 + r7, r1 - r7, i1 - i7, i1 + i7
    p3, q3, t3, s3 = r3 + r5, r3 - r5, i3 - i5, i3 + i5
    w, y = root * (p1 - p3), root * (t1 + t3)
    a1, b1 = q1 * big + q3 * small, s1 * small + s3 * big
    c1, d1 = q1 * small - q3 * big, s1 * big - s3 * small
    odd = [p1 + p3, a1 - b1, w - y, c1 - d1, t3 - t1, -(c1 + d1), -(w + y), -(a1 + b1)]
    return [even[c] + odd[c] for c in range(8)] + [even[c] - odd[c] for c in range(8)]


def window_start(first, slots):
    window = slots // 2 + PAD
    return pl.multiple_of(jnp.minimum(first // PAD * PAD, slots - window), PAD)


def prepare_kernel(counts_ref, samples_ref, targets_ref, own_ref, other_ref):
    device = lax.axis_index("dp")
    core = lax.rem(device, 2)
    slots, width = samples_ref.shape
    window = slots // 2 + PAD
    start = jnp.int32(0)
    for j in range(counts_ref.shape[0]):
        start = start + jnp.where(j < device, counts_ref[j], 0)
    cut = (start + counts_ref[device] + 1) // 2 - (start + 1) // 2
    late = window_start(cut, slots)
    lines = [targets_ref[i * width : (i + 1) * width].reshape(1, width) for i in range(slots // width)]
    lines.append(jnp.zeros((TAIL - len(lines), width), jnp.bfloat16))
    tail = jnp.concatenate(lines, axis=0)
    for target, is_late in ((own_ref, core), (other_ref, 1 - core)):
        begin = pl.multiple_of(late * is_late, PAD)
        target[:window, :] = samples_ref[pl.ds(begin, window), :]
        target[window:, :] = tail


def gather_rows(device, counts_ref, ends_ref, blocks, slots, loose, width, with_marks):
    core = lax.rem(device, 2)
    window = slots // 2 + PAD
    span = loose.shape[0]
    lane = lax.broadcasted_iota(jnp.int32, (8, span), 1)
    marks = jnp.zeros((8, span), jnp.float32)
    total = jnp.int32(0)
    for j in range(counts_ref.shape[0]):
        total = total + counts_ref[j]
        ends_ref[j] = total
    at = jnp.int32(0)
    for delta, block_ref in blocks:
        source = lax.bitwise_xor(device, delta)
        end = ends_ref[source]
        start = end - counts_ref[source]
        cut = (end + 1) // 2 - (start + 1) // 2
        share = jnp.where(core == 0, cut, end // 2 - start // 2)
        first = cut * core
        skip = first - window_start(cut, slots) * core
        base = at - skip + PAD
        spill = lax.rem(base, 8)
        begin = pl.multiple_of(base - spill, 8)
        block = block_ref[:window, :].astype(jnp.float32)
        block = jnp.concatenate([block, jnp.zeros((8, width), jnp.float32)], axis=0)
        block = pltpu.roll(block, spill, 0)
        edge = PAD + 8
        keep = lax.broadcasted_iota(jnp.int32, (edge, width), 0) < spill + skip
        loose[pl.ds(begin, edge), :] = jnp.where(keep, loose[pl.ds(begin, edge), :], block[:edge])
        loose[pl.ds(begin + edge, window + 8 - edge), :] = block[edge:]
        here, at = at, at + share
        if not with_marks:
            continue
        tail = block_ref[window:, :].astype(jnp.float32)
        line = jnp.concatenate([tail[i : i + 1, :] for i in range(slots // width)], axis=1)
        line = jnp.concatenate([line, jnp.zeros((1, span - slots), jnp.float32)], axis=1)
        line = pltpu.roll(jnp.broadcast_to(line, (8, span)), lax.rem(here - first + span, span), 1)
        marks = jnp.where((lane >= here) & (lane < at), line, marks)
    return marks


def main_kernel(deltas, first, final, counts_ref, *refs):
    count = len(deltas)
    blocks = list(zip(deltas, refs[:count]))
    high_table, low_table, ends_table, groups_table = refs[count : count + 4]
    if final:
        early = refs[count + 4] if first else None
        refs = refs[count + (5 if first else 4) :]
        own_ref, send_ref, kept = refs[0], refs[1], refs[-1]
        ends_ref, loose, rows2, rows_low, cube, spectra, products, sums_a, sums_b = refs[2:-1]
    else:
        kept, ends_ref, loose, rows2, rows_low, cube, spectra, products, sums_a, sums_b = refs[count + 4 :]
    sums = (sums_a, sums_b)
    device, panel = lax.axis_index("dp"), lax.axis_index("feat")
    pair_panel = device // 2
    n_groups = RADIX // 2
    width = rows2.shape[1]
    slots = 2 * (blocks[0][1].shape[0] - TAIL - PAD)
    rows = rows2.shape[0]
    pair_slots = 2 * SK // WIDE // lax.axis_size("dp")
    panel_slots = SK // WIDE // lax.axis_size("feat")
    junk = pair_slots + panel_slots

    marks = gather_rows(device, counts_ref, ends_ref, blocks, slots, loose, width, final)
    for t in range(rows // TILE):
        values = loose[PAD + first + t * TILE : PAD + first + (t + 1) * TILE, :]
        mean = jnp.sum(values * values, axis=1, keepdims=True) * (1.0 / width)
        factor = lax.rsqrt(mean + 1e-06) * width ** (-0.5)
        cube[t * TILE : (t + 1) * TILE, :] = jnp.broadcast_to(factor * factor * factor, (TILE, 128))
        rows2[t * TILE : (t + 1) * TILE, :] = values.astype(jnp.bfloat16)
        rows_low[t * TILE : (t + 1) * TILE, :] = values.astype(LOW)

    where_pair, where_panel = [], []
    for c in range(RADIX):
        low = c - pair_panel * pair_slots
        where_pair.append(jnp.where((low >= 0) & (low < pair_slots), low, junk))
        low = c - panel * panel_slots
        where_panel.append(jnp.where((low >= 0) & (low < panel_slots), low + pair_slots, junk))

    def forward(base, step):
        group, here = step % n_groups, pl.ds(base, TILE)
        spectra[step % 2] = jnp.dot(
            rows2[here, :], high_table[group], preferred_element_type=jnp.float32
        ) + jnp.dot(rows_low[here, :], low_table[group], preferred_element_type=jnp.float32)

    def multiply(base, step):
        group = step % n_groups
        source = spectra.at[step % 2]
        target = products.at[step % 2]
        chunk = 32
        for r in range(0, TILE, chunk):
            third = cube[pl.ds(base + r, chunk), :]
            for side in range(2):
                a_re, a_im, b_re, b_im, c_re, c_im = [
                    source[r : r + chunk, i * WIDE + side * HALF : i * WIDE + (side + 1) * HALF]
                    for i in range(6)
                ]
                a_re, a_im = a_re * third, a_im * third
                if group == 0 and side == 0:
                    real = a_re * b_re
                    both = a_im * b_im
                    m_re, m_im = real - both, a_re * b_im + a_im * b_re
                    first = lax.broadcasted_iota(jnp.int32, real.shape, 1) == 0
                    out_re = jnp.where(first, real * c_re, m_re * c_re - m_im * c_im)
                    out_im = jnp.where(first, both * c_im, m_re * c_im + m_im * c_re)
                else:
                    m_re, m_im = a_re * b_re - a_im * b_im, a_re * b_im + a_im * b_re
                    out_re = m_re * c_re - m_im * c_im
                    out_im = m_re * c_im + m_im * c_re
                if group == 0:
                    re_at, im_at = 2 * side * HALF, (2 * side + 1) * HALF
                else:
                    re_at, im_at = side * HALF, WIDE + side * HALF
                target[r : r + chunk, re_at : re_at + HALF] = out_re.astype(jnp.bfloat16)
                target[r : r + chunk, im_at : im_at + HALF] = out_im.astype(jnp.bfloat16)

    def inverse(step):
        group = step % n_groups
        source = products.at[step % 2]
        into = sums[step // n_groups]
        if group == 0:
            for side in range(2):
                at = slice(side * WIDE, (side + 1) * WIDE)
                into[:, at] = jnp.dot(source[:, at], ends_table[:, at], preferred_element_type=jnp.float32)
        else:
            into[:, 2 * group * WIDE : 2 * (group + 1) * WIDE] = jnp.dot(
                source[...], groups_table[group - 1], preferred_element_type=jnp.float32
            )

    def finish(source, base, part, parts):
        chunk = 16
        size = TILE // parts
        for r in range(part * size, (part + 1) * size, chunk):
            for side in range(2):
                outs = combine(
                    lambda i: source[r : r + chunk, i * WIDE + side * HALF : i * WIDE + (side + 1) * HALF]
                )
                at = slice(side * HALF, (side + 1) * HALF)
                for c in range(RADIX):
                    value = outs[c].astype(jnp.bfloat16)
                    kept[where_pair[c], pl.ds(base + r, chunk), at] = value
                    kept[where_panel[c], pl.ds(base + r, chunk), at] = value

    steps = 2 * n_groups

    def pair_step(t, _):
        bases = [pl.multiple_of(2 * t * TILE, TILE), pl.multiple_of((2 * t + 1) * TILE, TILE)]
        before = [pl.multiple_of(jnp.maximum(2 * t - 1, 1) * TILE, TILE), bases[0]]
        forward(bases[0], 0)
        for step in range(steps):
            if step + 1 < steps:
                forward(bases[(step + 1) // n_groups], step + 1)
            multiply(bases[step // n_groups], step)
            inverse(step)
            which = step // n_groups
            finish(sums[1 - which], before[which], step % n_groups, n_groups)
        return 0

    lax.fori_loop(0, rows // (2 * TILE), pair_step, 0)
    for part in range(n_groups):
        finish(sums[1], rows - TILE, part, n_groups)

    if not final:
        return
    odd = lax.rem(device, 2)
    each = pair_slots // 2
    marks = marks[:, : first + rows].astype(jnp.bfloat16)
    for i in range(each):
        for who, target in ((1 - odd, send_ref), (odd, own_ref)):
            left = kept[who * each + i].T
            left_early = early[who * each + i].T if first else None
            for j in range(panel_slots):
                block = jnp.dot(left, kept[pair_slots + j], preferred_element_type=jnp.float32)
                if first:
                    block += jnp.dot(left_early, early[pair_slots + j], preferred_element_type=jnp.float32)
                target[i * WIDE : (i + 1) * WIDE, j * WIDE : (j + 1) * WIDE] = block.astype(target.dtype)
    for j in range(panel_slots):
        line = jnp.dot(marks[:, first:], kept[pair_slots + j], preferred_element_type=jnp.float32)
        if first:
            line += jnp.dot(marks[:, :first], early[pair_slots + j], preferred_element_type=jnp.float32)
        at = slice(j * WIDE, (j + 1) * WIDE)
        own_ref[each * WIDE : each * WIDE + 8, at] = line
        send_ref[each * WIDE :, at] = jnp.concatenate([line, line], axis=0).astype(send_ref.dtype)


def merge_kernel(total, mine_ref, theirs_ref, mine_line_ref, theirs_line_ref, gram_ref, zty_ref):
    gram_ref[...] = (mine_ref[...] + theirs_ref[...].astype(jnp.float32)) * (1.0 / total)
    line = mine_line_ref[...] + theirs_line_ref[...].astype(jnp.float32)[:8]
    zty_ref[...] = line[:1] * total ** (-0.5)


def body(samples, targets, counts, bucket_ids, sign_bits):
    n_dp, n_feat = lax.axis_size("dp"), lax.axis_size("feat")
    slots, width = samples.shape
    half = slots // 2
    total = half * n_dp
    rows = total // 2
    scalars = [pl.BlockSpec(memory_space=pltpu.SMEM)]
    vector = pl.BlockSpec(memory_space=pltpu.VMEM)

    message = jax.ShapeDtypeStruct((half + PAD + TAIL, width), jnp.bfloat16)
    own, other = pl.pallas_call(
        prepare_kernel,
        out_shape=(message, message),
        in_specs=scalars + [vector] * 2,
        out_specs=(vector, vector),
        compiler_params=pltpu.CompilerParams(vmem_limit_bytes=VMEM_BYTES // 6),
    )(counts, samples, targets)

    def swap(block, bit):
        return lax.ppermute(block, "dp", [(i, i ^ bit) for i in range(n_dp)])

    high_table, low_table = forward_tables(bucket_ids, sign_bits)
    blocks = {0: own, 1: swap(other, 1)}
    near = [0, 1]
    for i in range(1, (n_dp - 1).bit_length()):
        for core in range(2):
            blocks[(1 << i) + core] = swap(other if core else own, (1 << i) + core)
            near.append((1 << i) + core)
    far = [delta for delta in range(n_dp) if delta not in blocks]
    sure = max(0, total - slots * len(far) - len(near)) // 2 if far else 0
    first = min(sure, rows // 3) // (2 * TILE) * 2 * TILE
    if first:
        high_table, sources = lax.optimization_barrier((high_table, dict(blocks)))
        blocks.update(sources)
    for delta in far:
        bits = [1 << i for i in range(1, n_dp.bit_length()) if delta >> i & 1]
        bit = bits[0] if delta % 2 else bits[-1]
        blocks[delta] = swap(blocks[delta ^ bit], bit)

    ends_table, group_table = inverse_tables()
    tables = (high_table, low_table, jnp.asarray(ends_table), jnp.asarray(group_table))
    own_columns, panel_columns = SK // n_dp, SK // n_feat
    kept_slots = 2 * own_columns // WIDE + panel_columns // WIDE + 1
    span = -(-(rows + half + 2 * PAD + 8) // 128) * 128

    def transform(deltas, begin, end, final, more):
        size = end - begin
        kept = (kept_slots, size, WIDE)
        out_shape = jax.ShapeDtypeStruct(kept, jnp.bfloat16)
        if final:
            out_shape = (
                jax.ShapeDtypeStruct((own_columns + 8, panel_columns), jnp.float32),
                jax.ShapeDtypeStruct((own_columns + 16, panel_columns), jnp.bfloat16),
            )
        scratch = [
            pltpu.SMEM((n_dp,), jnp.int32),
            pltpu.VMEM((span, width), jnp.float32),
            pltpu.VMEM((size, width), jnp.bfloat16),
            pltpu.VMEM((size, width), LOW),
            pltpu.VMEM((size, 128), jnp.float32),
            pltpu.VMEM((2, TILE, 6 * WIDE), jnp.float32),
            pltpu.VMEM((2, TILE, 2 * WIDE), jnp.bfloat16),
            pltpu.VMEM((TILE, SK), jnp.float32),
            pltpu.VMEM((TILE, SK), jnp.float32),
        ]
        return pl.pallas_call(
            functools.partial(main_kernel, deltas, begin, final),
            out_shape=out_shape,
            in_specs=scalars + [vector] * (len(deltas) + 4 + len(more)),
            out_specs=(vector, vector) if final else vector,
            scratch_shapes=scratch + ([pltpu.VMEM(kept, jnp.bfloat16)] if final else []),
            compiler_params=pltpu.CompilerParams(vmem_limit_bytes=VMEM_BYTES),
            cost_estimate=pl.CostEstimate(
                flops=2 * 10**7 * size, bytes_accessed=24 * 10**6, transcendentals=0
            ),
        )(counts, *[blocks[delta] for delta in deltas], *tables, *more)

    early = (transform(near, 0, first, False, ()),) if first else ()
    mine, send = transform(near + far, first, rows, True, early)
    theirs = swap(send, 1)
    blocks_in = min(own_columns, 2 * HALF)
    parts = own_columns // blocks_in
    rest = own_columns // 16
    gram, zty = pl.pallas_call(
        functools.partial(merge_kernel, total),
        grid=(parts,),
        out_shape=(
            jax.ShapeDtypeStruct((own_columns, panel_columns), jnp.float32),
            jax.ShapeDtypeStruct((1, panel_columns), jnp.float32),
        ),
        in_specs=[
            pl.BlockSpec((blocks_in, panel_columns), lambda i: (i, 0)),
            pl.BlockSpec((blocks_in, panel_columns), lambda i: (i, 0)),
            pl.BlockSpec((8, panel_columns), lambda i: (2 * rest, 0)),
            pl.BlockSpec((16, panel_columns), lambda i: (rest, 0)),
        ],
        out_specs=(
            pl.BlockSpec((blocks_in, panel_columns), lambda i: (i, 0)),
            pl.BlockSpec((1, panel_columns), lambda i: (0, 0)),
        ),
        compiler_params=pltpu.CompilerParams(vmem_limit_bytes=VMEM_BYTES // 2),
    )(mine, theirs, mine, theirs)
    return gram, zty.reshape(panel_columns)


def solution(mesh):
    placed = (P("dp", None), P("dp"), P(), P(), P())
    return jax.shard_map(
        body, mesh=mesh, in_specs=placed, out_specs=(P("dp", "feat"), P("feat")), check_vma=False
    )
```

```python
import functools
import math

import jax
import jax.numpy as jnp
import numpy as np
from jax import lax
from jax.experimental import pallas as pl
from jax.experimental.pallas import tpu as pltpu
from jax.sharding import PartitionSpec as P

SK = 4096
RADIX = 16
WIDE = SK // RADIX
HALF = WIDE // 2
TILE = 256
TAIL = 16
PAD = 16
LOW = jnp.float8_e5m2
VMEM_BYTES = 25 * 1024 * 1024


def three_terms(tables):
    terms = []
    for table in tables:
        rest = table.astype(np.float32)
        for _ in range(3):
            part = rest.astype(jnp.bfloat16)
            terms.append(part)
            rest = rest - part.astype(np.float32)
    return np.concatenate(terms, axis=1)


def turn_tables():
    groups = RADIX // 2
    first = np.arange(groups)
    second = np.where(first == 0, RADIX // 2, first + RADIX * HALF)
    starts = np.zeros(HALF, np.int64)
    starts[: 2 * groups] = np.concatenate([first, second])
    low, high = np.arange(WIDE)[:, None], np.arange(HALF)[:, None]
    angles = [
        low * np.arange(HALF)[None, :] % WIDE * (2.0 * np.pi / WIDE),
        low * starts[None, :] % SK * (2.0 * np.pi / SK),
        high * starts[None, :] % RADIX * (2.0 * np.pi / RADIX),
    ]
    pairs = [three_terms([np.cos(angle), -np.sin(angle)]) for angle in angles]
    high_part = np.pad(pairs[2], ((0, 0), (0, 6 * HALF)))
    return np.concatenate([np.concatenate(pairs[:2], axis=1), high_part], axis=0)


def inverse_tables():
    scale = SK ** (-0.5)
    column = np.arange(WIDE)[None, :]

    def trig(freq):
        angle = (freq[:, None] * column % SK) * (2.0 * np.pi / SK)
        return 2.0 * scale * np.cos(angle), 2.0 * scale * np.sin(angle)

    narrow = np.arange(HALF)
    cos_a, sin_a = trig(RADIX * narrow)
    cos_b, sin_b = trig(RADIX // 2 + RADIX * narrow)
    imag_a = -sin_a
    cos_a[0] = scale
    imag_a[0] = scale * (1.0 - 2.0 * (np.arange(WIDE) % 2))
    ends = np.concatenate(
        [np.concatenate([cos_a, imag_a], axis=0), np.concatenate([cos_b, -sin_b], axis=0)], axis=1
    )
    groups = []
    for group in range(1, RADIX // 2):
        cosine, sine = trig(group + RADIX * np.arange(WIDE))
        groups.append(
            np.concatenate(
                [np.concatenate([cosine, sine], axis=1), np.concatenate([-sine, cosine], axis=1)],
                axis=0,
            )
        )
    return ends.astype(jnp.bfloat16), np.stack(groups).astype(jnp.bfloat16)


def table_kernel(packed_ref, turns_ref, high_ref, low_ref):
    sketches, features_in = packed_ref.shape
    groups = RADIX // 2
    blank = jnp.zeros((8 - sketches, features_in), jnp.float32)
    columns = jnp.concatenate([packed_ref[...].astype(jnp.float32), blank], axis=0).T

    def three(full, at):
        return full[:, at : at + HALF] + full[:, at + HALF : at + 2 * HALF] + full[:, at + 2 * HALF : at + 3 * HALF]

    chunk = 64
    for k in range(sketches):
        packed = columns[:, k : k + 1].astype(jnp.int32)
        bucket = packed // 2
        sign = (2 * (packed % 2) - 1).astype(jnp.float32)
        lane = lax.broadcasted_iota(jnp.int32, (features_in, WIDE), 1)
        chosen = jnp.where(bucket % WIDE == lane, 1.0, 0.0).astype(jnp.bfloat16)
        full = jnp.dot(chosen, turns_ref[:WIDE, :], preferred_element_type=jnp.float32)
        base_re, base_im, fine_re, fine_im = [three(full, 3 * i * HALF) for i in range(4)]
        lane = lax.broadcasted_iota(jnp.int32, (features_in, HALF), 1)
        chosen = jnp.where(bucket // WIDE == lane, 1.0, 0.0).astype(jnp.bfloat16)
        full = jnp.dot(chosen, turns_ref[WIDE:, : 6 * HALF], preferred_element_type=jnp.float32)
        wide_re, wide_im = three(full, 0), three(full, 3 * HALF)
        turns_re = (fine_re * wide_re - fine_im * wide_im) * sign
        turns_im = (fine_re * wide_im + fine_im * wide_re) * sign
        middle = sign * (1 - 2 * (bucket % 2)).astype(jnp.float32)
        for r in range(0, features_in, chunk):
            rows = slice(r, r + chunk)
            first_lane = lax.broadcasted_iota(jnp.int32, (chunk, HALF), 1) == 0
            for group in range(groups):
                for side in range(2):
                    at = side * groups + group
                    turn_re, turn_im = turns_re[rows, at : at + 1], turns_im[rows, at : at + 1]
                    real = turn_re * base_re[rows] - turn_im * base_im[rows]
                    imag = turn_re * base_im[rows] + turn_im * base_re[rows]
                    if group == 0 and side == 0:
                        imag = jnp.where(first_lane, middle[rows], imag)
                    for part, values in enumerate((real, imag)):
                        start = (2 * k + part) * WIDE + side * HALF
                        high = values.astype(jnp.bfloat16)
                        high_ref[group, rows, start : start + HALF] = high
                        low_ref[group, rows, start : start + HALF] = (
                            values - high.astype(jnp.float32)
                        ).astype(LOW)


def forward_tables(bucket_ids, sign_bits):
    shape = (RADIX // 2, bucket_ids.shape[1], 6 * WIDE)
    packed = 2 * bucket_ids + sign_bits
    vector = pl.BlockSpec(memory_space=pltpu.VMEM)
    return pl.pallas_call(
        table_kernel,
        out_shape=(jax.ShapeDtypeStruct(shape, jnp.bfloat16), jax.ShapeDtypeStruct(shape, LOW)),
        in_specs=[vector] * 2,
        out_specs=(vector, vector),
        compiler_params=pltpu.CompilerParams(vmem_limit_bytes=VMEM_BYTES // 2),
        cost_estimate=pl.CostEstimate(flops=2 * 10**9, bytes_accessed=14 * 10**6, transcendentals=0),
    )(packed, jnp.asarray(turn_tables()))


def combine(load):
    root = math.sqrt(0.5)
    big, small = math.cos(math.pi / 8), math.sin(math.pi / 8)
    r4, i4 = load(8), load(9)
    q0, q8 = load(0), load(1)
    a, b = q0 + q8, q0 - q8
    quarter = (a + r4, b - i4, a - r4, b + i4)
    r2, i2, r6, i6 = load(4), load(5), load(12), load(13)
    u, v = r2 - r6, i2 + i6
    other = (r2 + r6, root * (u - v), i6 - i2, -root * (u + v))
    even = [quarter[c] + other[c] for c in range(4)] + [quarter[c] - other[c] for c in range(4)]
    r1, i1, r7, i7 = load(2), load(3), load(14), load(15)
    r3, i3, r5, i5 = load(6), load(7), load(10), load(11)
    p1, q1, t1, s1 = r1 + r7, r1 - r7, i1 - i7, i1 + i7
    p3, q3, t3, s3 = r3 + r5, r3 - r5, i3 - i5, i3 + i5
    w, y = root * (p1 - p3), root * (t1 + t3)
    a1, b1 = q1 * big + q3 * small, s1 * small + s3 * big
    c1, d1 = q1 * small - q3 * big, s1 * big - s3 * small
    odd = [p1 + p3, a1 - b1, w - y, c1 - d1, t3 - t1, -(c1 + d1), -(w + y), -(a1 + b1)]
    return [even[c] + odd[c] for c in range(8)] + [even[c] - odd[c] for c in range(8)]


def window_start(first, slots):
    window = slots // 2 + PAD
    return pl.multiple_of(jnp.minimum(first // PAD * PAD, slots - window), PAD)


def prepare_kernel(counts_ref, samples_ref, targets_ref, own_ref, other_ref):
    device = lax.axis_index("dp")
    core = lax.rem(device, 2)
    slots, width = samples_ref.shape
    window = slots // 2 + PAD
    start = jnp.int32(0)
    for j in range(counts_ref.shape[0]):
        start = start + jnp.where(j < device, counts_ref[j], 0)
    cut = (start + counts_ref[device] + 1) // 2 - (start + 1) // 2
    late = window_start(cut, slots)
    lines = [targets_ref[i * width : (i + 1) * width].reshape(1, width) for i in range(slots // width)]
    lines.append(jnp.zeros((TAIL - len(lines), width), jnp.bfloat16))
    tail = jnp.concatenate(lines, axis=0)
    for target, is_late in ((own_ref, core), (other_ref, 1 - core)):
        begin = pl.multiple_of(late * is_late, PAD)
        target[:window, :] = samples_ref[pl.ds(begin, window), :]
        target[window:, :] = tail


def gather_rows(device, counts_ref, ends_ref, blocks, slots, loose, width, with_marks):
    core = lax.rem(device, 2)
    window = slots // 2 + PAD
    span = loose.shape[0]
    lane = lax.broadcasted_iota(jnp.int32, (8, span), 1)
    marks = jnp.zeros((8, span), jnp.float32)
    total = jnp.int32(0)
    for j in range(counts_ref.shape[0]):
        total = total + counts_ref[j]
        ends_ref[j] = total
    at = jnp.int32(0)
    for delta, block_ref in blocks:
        source = lax.bitwise_xor(device, delta)
        end = ends_ref[source]
        start = end - counts_ref[source]
        cut = (end + 1) // 2 - (start + 1) // 2
        share = jnp.where(core == 0, cut, end // 2 - start // 2)
        first = cut * core
        skip = first - window_start(cut, slots) * core
        base = at - skip + PAD
        spill = lax.rem(base, 8)
        begin = pl.multiple_of(base - spill, 8)
        block = block_ref[:window, :].astype(jnp.float32)
        block = jnp.concatenate([block, jnp.zeros((8, width), jnp.float32)], axis=0)
        block = pltpu.roll(block, spill, 0)
        edge = PAD + 8
        keep = lax.broadcasted_iota(jnp.int32, (edge, width), 0) < spill + skip
        loose[pl.ds(begin, edge), :] = jnp.where(keep, loose[pl.ds(begin, edge), :], block[:edge])
        loose[pl.ds(begin + edge, window + 8 - edge), :] = block[edge:]
        here, at = at, at + share
        if not with_marks:
            continue
        tail = block_ref[window:, :].astype(jnp.float32)
        line = jnp.concatenate([tail[i : i + 1, :] for i in range(slots // width)], axis=1)
        line = jnp.concatenate([line, jnp.zeros((1, span - slots), jnp.float32)], axis=1)
        line = pltpu.roll(jnp.broadcast_to(line, (8, span)), lax.rem(here - first + span, span), 1)
        marks = jnp.where((lane >= here) & (lane < at), line, marks)
    return marks


def main_kernel(deltas, first, final, counts_ref, *refs):
    count = len(deltas)
    blocks = list(zip(deltas, refs[:count]))
    high_table, low_table, ends_table, groups_table = refs[count : count + 4]
    if final:
        early = refs[count + 4] if first else None
        refs = refs[count + (5 if first else 4) :]
        own_ref, send_ref, kept = refs[0], refs[1], refs[-1]
        ends_ref, loose, rows2, rows_low, cube, spectra, products, sums_a, sums_b = refs[2:-1]
    else:
        kept, ends_ref, loose, rows2, rows_low, cube, spectra, products, sums_a, sums_b = refs[count + 4 :]
    sums = (sums_a, sums_b)
    device, panel = lax.axis_index("dp"), lax.axis_index("feat")
    pair_panel = device // 2
    n_groups = RADIX // 2
    width = rows2.shape[1]
    slots = 2 * (blocks[0][1].shape[0] - TAIL - PAD)
    rows = rows2.shape[0]
    pair_slots = 2 * SK // WIDE // lax.axis_size("dp")
    panel_slots = SK // WIDE // lax.axis_size("feat")
    junk = pair_slots + panel_slots

    marks = gather_rows(device, counts_ref, ends_ref, blocks, slots, loose, width, final)
    for t in range(rows // TILE):
        values = loose[PAD + first + t * TILE : PAD + first + (t + 1) * TILE, :]
        mean = jnp.sum(values * values, axis=1, keepdims=True) * (1.0 / width)
        factor = lax.rsqrt(mean + 1e-06) * width ** (-0.5)
        cube[t * TILE : (t + 1) * TILE, :] = jnp.broadcast_to(factor * factor * factor, (TILE, 128))
        rows2[t * TILE : (t + 1) * TILE, :] = values.astype(jnp.bfloat16)
        rows_low[t * TILE : (t + 1) * TILE, :] = values.astype(LOW)

    where_pair, where_panel = [], []
    for c in range(RADIX):
        low = c - pair_panel * pair_slots
        where_pair.append(jnp.where((low >= 0) & (low < pair_slots), low, junk))
        low = c - panel * panel_slots
        where_panel.append(jnp.where((low >= 0) & (low < panel_slots), low + pair_slots, junk))

    def forward(base, step):
        group, here = step % n_groups, pl.ds(base, TILE)
        spectra[step % 2] = jnp.dot(
            rows2[here, :], high_table[group], preferred_element_type=jnp.float32
        ) + jnp.dot(rows_low[here, :], low_table[group], preferred_element_type=jnp.float32)

    def multiply(base, step):
        group = step % n_groups
        source = spectra.at[step % 2]
        target = products.at[step % 2]
        chunk = 32
        for r in range(0, TILE, chunk):
            third = cube[pl.ds(base + r, chunk), :]
            for side in range(2):
                a_re, a_im, b_re, b_im, c_re, c_im = [
                    source[r : r + chunk, i * WIDE + side * HALF : i * WIDE + (side + 1) * HALF]
                    for i in range(6)
                ]
                a_re, a_im = a_re * third, a_im * third
                if group == 0 and side == 0:
                    real = a_re * b_re
                    both = a_im * b_im
                    m_re, m_im = real - both, a_re * b_im + a_im * b_re
                    first = lax.broadcasted_iota(jnp.int32, real.shape, 1) == 0
                    out_re = jnp.where(first, real * c_re, m_re * c_re - m_im * c_im)
                    out_im = jnp.where(first, both * c_im, m_re * c_im + m_im * c_re)
                else:
                    m_re, m_im = a_re * b_re - a_im * b_im, a_re * b_im + a_im * b_re
                    out_re = m_re * c_re - m_im * c_im
                    out_im = m_re * c_im + m_im * c_re
                if group == 0:
                    re_at, im_at = 2 * side * HALF, (2 * side + 1) * HALF
                else:
                    re_at, im_at = side * HALF, WIDE + side * HALF
                target[r : r + chunk, re_at : re_at + HALF] = out_re.astype(jnp.bfloat16)
                target[r : r + chunk, im_at : im_at + HALF] = out_im.astype(jnp.bfloat16)

    def inverse(step):
        group = step % n_groups
        source = products.at[step % 2]
        into = sums[step // n_groups]
        if group == 0:
            for side in range(2):
                at = slice(side * WIDE, (side + 1) * WIDE)
                into[:, at] = jnp.dot(source[:, at], ends_table[:, at], preferred_element_type=jnp.float32)
        else:
            into[:, 2 * group * WIDE : 2 * (group + 1) * WIDE] = jnp.dot(
                source[...], groups_table[group - 1], preferred_element_type=jnp.float32
            )

    def finish(source, base, part, parts):
        chunk = 16
        size = TILE // parts
        for r in range(part * size, (part + 1) * size, chunk):
            for side in range(2):
                outs = combine(
                    lambda i: source[r : r + chunk, i * WIDE + side * HALF : i * WIDE + (side + 1) * HALF]
                )
                at = slice(side * HALF, (side + 1) * HALF)
                for c in range(RADIX):
                    value = outs[c].astype(jnp.bfloat16)
                    kept[where_pair[c], pl.ds(base + r, chunk), at] = value
                    kept[where_panel[c], pl.ds(base + r, chunk), at] = value

    steps = 2 * n_groups

    def pair_step(t, _):
        bases = [pl.multiple_of(2 * t * TILE, TILE), pl.multiple_of((2 * t + 1) * TILE, TILE)]
        before = [pl.multiple_of(jnp.maximum(2 * t - 1, 1) * TILE, TILE), bases[0]]
        forward(bases[0], 0)
        for step in range(steps):
            if step + 1 < steps:
                forward(bases[(step + 1) // n_groups], step + 1)
            multiply(bases[step // n_groups], step)
            inverse(step)
            which = step // n_groups
            finish(sums[1 - which], before[which], step % n_groups, n_groups)
        return 0

    lax.fori_loop(0, rows // (2 * TILE), pair_step, 0)
    for part in range(n_groups):
        finish(sums[1], rows - TILE, part, n_groups)

    if not final:
        return
    odd = lax.rem(device, 2)
    each = pair_slots // 2
    marks = marks[:, : first + rows].astype(jnp.bfloat16)
    for i in range(each):
        for who, target in ((1 - odd, send_ref), (odd, own_ref)):
            left = kept[who * each + i].T
            left_early = early[who * each + i].T if first else None
            for j in range(panel_slots):
                block = jnp.dot(left, kept[pair_slots + j], preferred_element_type=jnp.float32)
                if first:
                    block += jnp.dot(left_early, early[pair_slots + j], preferred_element_type=jnp.float32)
                target[i * WIDE : (i + 1) * WIDE, j * WIDE : (j + 1) * WIDE] = block.astype(target.dtype)
    for j in range(panel_slots):
        line = jnp.dot(marks[:, first:], kept[pair_slots + j], preferred_element_type=jnp.float32)
        if first:
            line += jnp.dot(marks[:, :first], early[pair_slots + j], preferred_element_type=jnp.float32)
        at = slice(j * WIDE, (j + 1) * WIDE)
        own_ref[each * WIDE : each * WIDE + 8, at] = line
        send_ref[each * WIDE :, at] = jnp.concatenate([line, line], axis=0).astype(send_ref.dtype)


def merge_kernel(total, mine_ref, theirs_ref, mine_line_ref, theirs_line_ref, gram_ref, zty_ref):
    gram_ref[...] = (mine_ref[...] + theirs_ref[...].astype(jnp.float32)) * (1.0 / total)
    line = mine_line_ref[...] + theirs_line_ref[...].astype(jnp.float32)[:8]
    zty_ref[...] = line[:1] * total ** (-0.5)


def body(samples, targets, counts, bucket_ids, sign_bits):
    n_dp, n_feat = lax.axis_size("dp"), lax.axis_size("feat")
    slots, width = samples.shape
    half = slots // 2
    total = half * n_dp
    rows = total // 2
    scalars = [pl.BlockSpec(memory_space=pltpu.SMEM)]
    vector = pl.BlockSpec(memory_space=pltpu.VMEM)

    message = jax.ShapeDtypeStruct((half + PAD + TAIL, width), jnp.bfloat16)
    own, other = pl.pallas_call(
        prepare_kernel,
        out_shape=(message, message),
        in_specs=scalars + [vector] * 2,
        out_specs=(vector, vector),
    )(counts, samples, targets)

    def swap(block, bit):
        return lax.ppermute(block, "dp", [(i, i ^ bit) for i in range(n_dp)])

    high_table, low_table = forward_tables(bucket_ids, sign_bits)
    blocks = {0: own, 1: swap(other, 1)}
    near = [0, 1]
    for i in range(1, (n_dp - 1).bit_length()):
        for core in range(2):
            blocks[(1 << i) + core] = swap(other if core else own, (1 << i) + core)
            near.append((1 << i) + core)
    far = [delta for delta in range(n_dp) if delta not in blocks]
    sure = max(0, total - slots * len(far) - len(near)) // 2 if far else 0
    first = min(sure, rows // 3) // (2 * TILE) * 2 * TILE
    if first:
        high_table, sources = lax.optimization_barrier((high_table, dict(blocks)))
        blocks.update(sources)
    for delta in far:
        bits = [1 << i for i in range(1, n_dp.bit_length()) if delta >> i & 1]
        bit = bits[0] if delta % 2 else bits[-1]
        blocks[delta] = swap(blocks[delta ^ bit], bit)

    ends_table, group_table = inverse_tables()
    tables = (high_table, low_table, jnp.asarray(ends_table), jnp.asarray(group_table))
    own_columns, panel_columns = SK // n_dp, SK // n_feat
    kept_slots = 2 * own_columns // WIDE + panel_columns // WIDE + 1
    span = -(-(rows + half + 2 * PAD + 8) // 128) * 128

    def transform(deltas, begin, end, final, more):
        size = end - begin
        kept = (kept_slots, size, WIDE)
        out_shape = jax.ShapeDtypeStruct(kept, jnp.bfloat16)
        if final:
            out_shape = (
                jax.ShapeDtypeStruct((own_columns + 8, panel_columns), jnp.float32),
                jax.ShapeDtypeStruct((own_columns + 16, panel_columns), jnp.bfloat16),
            )
        scratch = [
            pltpu.SMEM((n_dp,), jnp.int32),
            pltpu.VMEM((span, width), jnp.float32),
            pltpu.VMEM((size, width), jnp.bfloat16),
            pltpu.VMEM((size, width), LOW),
            pltpu.VMEM((size, 128), jnp.float32),
            pltpu.VMEM((2, TILE, 6 * WIDE), jnp.float32),
            pltpu.VMEM((2, TILE, 2 * WIDE), jnp.bfloat16),
            pltpu.VMEM((TILE, SK), jnp.float32),
            pltpu.VMEM((TILE, SK), jnp.float32),
        ]
        return pl.pallas_call(
            functools.partial(main_kernel, deltas, begin, final),
            out_shape=out_shape,
            in_specs=scalars + [vector] * (len(deltas) + 4 + len(more)),
            out_specs=(vector, vector) if final else vector,
            scratch_shapes=scratch + ([pltpu.VMEM(kept, jnp.bfloat16)] if final else []),
            compiler_params=pltpu.CompilerParams(vmem_limit_bytes=VMEM_BYTES),
            cost_estimate=pl.CostEstimate(
                flops=2 * 10**7 * size, bytes_accessed=24 * 10**6, transcendentals=0
            ),
        )(counts, *[blocks[delta] for delta in deltas], *tables, *more)

    early = (transform(near, 0, first, False, ()),) if first else ()
    mine, send = transform(near + far, first, rows, True, early)
    theirs = swap(send, 1)
    blocks_in = min(own_columns, 2 * HALF)
    parts = own_columns // blocks_in
    rest = own_columns // 16
    gram, zty = pl.pallas_call(
        functools.partial(merge_kernel, total),
        grid=(parts,),
        out_shape=(
            jax.ShapeDtypeStruct((own_columns, panel_columns), jnp.float32),
            jax.ShapeDtypeStruct((1, panel_columns), jnp.float32),
        ),
        in_specs=[
            pl.BlockSpec((blocks_in, panel_columns), lambda i: (i, 0)),
            pl.BlockSpec((blocks_in, panel_columns), lambda i: (i, 0)),
            pl.BlockSpec((8, panel_columns), lambda i: (2 * rest, 0)),
            pl.BlockSpec((16, panel_columns), lambda i: (rest, 0)),
        ],
        out_specs=(
            pl.BlockSpec((blocks_in, panel_columns), lambda i: (i, 0)),
            pl.BlockSpec((1, panel_columns), lambda i: (0, 0)),
        ),
        compiler_params=pltpu.CompilerParams(vmem_limit_bytes=VMEM_BYTES // 2),
    )(mine, theirs, mine, theirs)
    return gram, zty.reshape(panel_columns)


def solution(mesh):
    placed = (P("dp", None), P("dp"), P(), P(), P())
    return jax.shard_map(
        body, mesh=mesh, in_specs=placed, out_specs=(P("dp", "feat"), P("feat")), check_vma=False
    )
```

```python
import functools
import math

import jax
import jax.numpy as jnp
import numpy as np
from jax import lax
from jax.experimental import pallas as pl
from jax.experimental.pallas import tpu as pltpu
from jax.sharding import PartitionSpec as P

SK = 4096
RADIX = 16
WIDE = SK // RADIX
HALF = WIDE // 2
TILE = 256
TAIL = 16
PAD = 16
LOW = jnp.float8_e5m2
VMEM_BYTES = 25 * 1024 * 1024


def two_terms(tables):
    terms = []
    for table in tables:
        rest = table.astype(np.float32)
        for _ in range(2):
            part = rest.astype(jnp.bfloat16)
            terms.append(part)
            rest = rest - part.astype(np.float32)
    return np.concatenate(terms, axis=1)


def turn_tables():
    groups = RADIX // 2
    first = np.arange(groups)
    second = np.where(first == 0, RADIX // 2, first + RADIX * HALF)
    starts = np.zeros(HALF, np.int64)
    starts[: 2 * groups] = np.concatenate([first, second])
    low, high = np.arange(WIDE)[:, None], np.arange(HALF)[:, None]
    angles = [
        low * np.arange(HALF)[None, :] % WIDE * (2.0 * np.pi / WIDE),
        low * starts[None, :] % SK * (2.0 * np.pi / SK),
        high * starts[None, :] % RADIX * (2.0 * np.pi / RADIX),
    ]
    pairs = [two_terms([np.cos(angle), -np.sin(angle)]) for angle in angles]
    high_part = np.pad(pairs[2], ((0, 0), (0, 4 * HALF)))
    return np.concatenate([np.concatenate(pairs[:2], axis=1), high_part], axis=0)


def inverse_tables():
    scale = SK ** (-0.5)
    column = np.arange(WIDE)[None, :]

    def trig(freq):
        angle = (freq[:, None] * column % SK) * (2.0 * np.pi / SK)
        return 2.0 * scale * np.cos(angle), 2.0 * scale * np.sin(angle)

    narrow = np.arange(HALF)
    cos_a, sin_a = trig(RADIX * narrow)
    cos_b, sin_b = trig(RADIX // 2 + RADIX * narrow)
    imag_a = -sin_a
    cos_a[0] = scale
    imag_a[0] = scale * (1.0 - 2.0 * (np.arange(WIDE) % 2))
    ends = np.concatenate(
        [np.concatenate([cos_a, imag_a], axis=0), np.concatenate([cos_b, -sin_b], axis=0)], axis=1
    )
    groups = []
    for group in range(1, RADIX // 2):
        cosine, sine = trig(group + RADIX * np.arange(WIDE))
        groups.append(
            np.concatenate(
                [np.concatenate([cosine, sine], axis=1), np.concatenate([-sine, cosine], axis=1)],
                axis=0,
            )
        )
    return ends.astype(jnp.bfloat16), np.stack(groups).astype(jnp.bfloat16)


def table_kernel(packed_ref, turns_ref, high_ref, low_ref):
    sketches, features_in = packed_ref.shape
    groups = RADIX // 2
    blank = jnp.zeros((8 - sketches, features_in), jnp.float32)
    columns = jnp.concatenate([packed_ref[...].astype(jnp.float32), blank], axis=0).T

    def join(full, at):
        return full[:, at : at + HALF] + full[:, at + HALF : at + 2 * HALF]

    chunk = 64
    for k in range(sketches):
        packed = columns[:, k : k + 1].astype(jnp.int32)
        bucket = packed // 2
        sign = (2 * (packed % 2) - 1).astype(jnp.float32)
        lane = lax.broadcasted_iota(jnp.int32, (features_in, WIDE), 1)
        chosen = jnp.where(bucket % WIDE == lane, 1.0, 0.0).astype(jnp.bfloat16)
        full = jnp.dot(chosen, turns_ref[:WIDE, :], preferred_element_type=jnp.float32)
        base_re, base_im, fine_re, fine_im = [join(full, 2 * i * HALF) for i in range(4)]
        lane = lax.broadcasted_iota(jnp.int32, (features_in, HALF), 1)
        chosen = jnp.where(bucket // WIDE == lane, 1.0, 0.0).astype(jnp.bfloat16)
        full = jnp.dot(chosen, turns_ref[WIDE:, : 4 * HALF], preferred_element_type=jnp.float32)
        wide_re, wide_im = join(full, 0), join(full, 2 * HALF)
        turns_re = (fine_re * wide_re - fine_im * wide_im) * sign
        turns_im = (fine_re * wide_im + fine_im * wide_re) * sign
        middle = sign * (1 - 2 * (bucket % 2)).astype(jnp.float32)
        for r in range(0, features_in, chunk):
            rows = slice(r, r + chunk)
            first_lane = lax.broadcasted_iota(jnp.int32, (chunk, HALF), 1) == 0
            for group in range(groups):
                for side in range(2):
                    at = side * groups + group
                    turn_re, turn_im = turns_re[rows, at : at + 1], turns_im[rows, at : at + 1]
                    real = turn_re * base_re[rows] - turn_im * base_im[rows]
                    imag = turn_re * base_im[rows] + turn_im * base_re[rows]
                    if group == 0 and side == 0:
                        imag = jnp.where(first_lane, middle[rows], imag)
                    for part, values in enumerate((real, imag)):
                        start = (2 * k + part) * WIDE + side * HALF
                        high = values.astype(jnp.bfloat16)
                        high_ref[group, rows, start : start + HALF] = high
                        low_ref[group, rows, start : start + HALF] = (
                            values - high.astype(jnp.float32)
                        ).astype(LOW)


def forward_tables(bucket_ids, sign_bits):
    shape = (RADIX // 2, bucket_ids.shape[1], 6 * WIDE)
    packed = 2 * bucket_ids + sign_bits
    vector = pl.BlockSpec(memory_space=pltpu.VMEM)
    return pl.pallas_call(
        table_kernel,
        out_shape=(jax.ShapeDtypeStruct(shape, jnp.bfloat16), jax.ShapeDtypeStruct(shape, LOW)),
        in_specs=[vector] * 2,
        out_specs=(vector, vector),
        compiler_params=pltpu.CompilerParams(vmem_limit_bytes=VMEM_BYTES // 2),
        cost_estimate=pl.CostEstimate(flops=2 * 10**9, bytes_accessed=14 * 10**6, transcendentals=0),
    )(packed, jnp.asarray(turn_tables()))


def combine(load):
    root = math.sqrt(0.5)
    big, small = math.cos(math.pi / 8), math.sin(math.pi / 8)
    r4, i4 = load(8), load(9)
    q0, q8 = load(0), load(1)
    a, b = q0 + q8, q0 - q8
    quarter = (a + r4, b - i4, a - r4, b + i4)
    r2, i2, r6, i6 = load(4), load(5), load(12), load(13)
    u, v = r2 - r6, i2 + i6
    other = (r2 + r6, root * (u - v), i6 - i2, -root * (u + v))
    even = [quarter[c] + other[c] for c in range(4)] + [quarter[c] - other[c] for c in range(4)]
    r1, i1, r7, i7 = load(2), load(3), load(14), load(15)
    r3, i3, r5, i5 = load(6), load(7), load(10), load(11)
    p1, q1, t1, s1 = r1 + r7, r1 - r7, i1 - i7, i1 + i7
    p3, q3, t3, s3 = r3 + r5, r3 - r5, i3 - i5, i3 + i5
    w, y = root * (p1 - p3), root * (t1 + t3)
    a1, b1 = q1 * big + q3 * small, s1 * small + s3 * big
    c1, d1 = q1 * small - q3 * big, s1 * big - s3 * small
    odd = [p1 + p3, a1 - b1, w - y, c1 - d1, t3 - t1, -(c1 + d1), -(w + y), -(a1 + b1)]
    return [even[c] + odd[c] for c in range(8)] + [even[c] - odd[c] for c in range(8)]


def window_start(first, slots):
    window = slots // 2 + PAD
    return pl.multiple_of(jnp.minimum(first // PAD * PAD, slots - window), PAD)


def prepare_kernel(counts_ref, samples_ref, targets_ref, own_ref, other_ref):
    device = lax.axis_index("dp")
    core = lax.rem(device, 2)
    slots, width = samples_ref.shape
    window = slots // 2 + PAD
    start = jnp.int32(0)
    for j in range(counts_ref.shape[0]):
        start = start + jnp.where(j < device, counts_ref[j], 0)
    cut = (start + counts_ref[device] + 1) // 2 - (start + 1) // 2
    late = window_start(cut, slots)
    lines = [targets_ref[i * width : (i + 1) * width].reshape(1, width) for i in range(slots // width)]
    lines.append(jnp.zeros((TAIL - len(lines), width), jnp.bfloat16))
    tail = jnp.concatenate(lines, axis=0)
    for target, is_late in ((own_ref, core), (other_ref, 1 - core)):
        begin = pl.multiple_of(late * is_late, PAD)
        target[:window, :] = samples_ref[pl.ds(begin, window), :]
        target[window:, :] = tail


def gather_rows(device, counts_ref, ends_ref, blocks, slots, loose, width, with_marks):
    core = lax.rem(device, 2)
    window = slots // 2 + PAD
    span = loose.shape[0]
    lane = lax.broadcasted_iota(jnp.int32, (8, span), 1)
    marks = jnp.zeros((8, span), jnp.float32)
    total = jnp.int32(0)
    for j in range(counts_ref.shape[0]):
        total = total + counts_ref[j]
        ends_ref[j] = total
    at = jnp.int32(0)
    for delta, block_ref in blocks:
        source = lax.bitwise_xor(device, delta)
        end = ends_ref[source]
        start = end - counts_ref[source]
        cut = (end + 1) // 2 - (start + 1) // 2
        share = jnp.where(core == 0, cut, end // 2 - start // 2)
        first = cut * core
        skip = first - window_start(cut, slots) * core
        base = at - skip + PAD
        spill = lax.rem(base, 8)
        begin = pl.multiple_of(base - spill, 8)
        block = block_ref[:window, :].astype(jnp.float32)
        block = jnp.concatenate([block, jnp.zeros((8, width), jnp.float32)], axis=0)
        block = pltpu.roll(block, spill, 0)
        edge = PAD + 8
        keep = lax.broadcasted_iota(jnp.int32, (edge, width), 0) < spill + skip
        loose[pl.ds(begin, edge), :] = jnp.where(keep, loose[pl.ds(begin, edge), :], block[:edge])
        loose[pl.ds(begin + edge, window + 8 - edge), :] = block[edge:]
        here, at = at, at + share
        if not with_marks:
            continue
        tail = block_ref[window:, :].astype(jnp.float32)
        line = jnp.concatenate([tail[i : i + 1, :] for i in range(slots // width)], axis=1)
        line = jnp.concatenate([line, jnp.zeros((1, span - slots), jnp.float32)], axis=1)
        line = pltpu.roll(jnp.broadcast_to(line, (8, span)), lax.rem(here - first + span, span), 1)
        marks = jnp.where((lane >= here) & (lane < at), line, marks)
    return marks


def main_kernel(deltas, first, final, counts_ref, *refs):
    count = len(deltas)
    blocks = list(zip(deltas, refs[:count]))
    high_table, low_table, ends_table, groups_table = refs[count : count + 4]
    if final:
        early = refs[count + 4] if first else None
        refs = refs[count + (5 if first else 4) :]
        own_ref, send_ref, kept = refs[0], refs[1], refs[-1]
        ends_ref, loose, rows2, rows_low, cube, spectra, products, sums_a, sums_b = refs[2:-1]
    else:
        kept, ends_ref, loose, rows2, rows_low, cube, spectra, products, sums_a, sums_b = refs[count + 4 :]
    sums = (sums_a, sums_b)
    device, panel = lax.axis_index("dp"), lax.axis_index("feat")
    pair_panel = device // 2
    n_groups = RADIX // 2
    width = rows2.shape[1]
    slots = 2 * (blocks[0][1].shape[0] - TAIL - PAD)
    rows = rows2.shape[0]
    pair_slots = 2 * SK // WIDE // lax.axis_size("dp")
    panel_slots = SK // WIDE // lax.axis_size("feat")
    junk = pair_slots + panel_slots

    marks = gather_rows(device, counts_ref, ends_ref, blocks, slots, loose, width, final)
    for t in range(rows // TILE):
        values = loose[PAD + first + t * TILE : PAD + first + (t + 1) * TILE, :]
        mean = jnp.sum(values * values, axis=1, keepdims=True) * (1.0 / width)
        factor = lax.rsqrt(mean + 1e-06) * width ** (-0.5)
        cube[t * TILE : (t + 1) * TILE, :] = jnp.broadcast_to(factor * factor * factor, (TILE, 128))
        rows2[t * TILE : (t + 1) * TILE, :] = values.astype(jnp.bfloat16)
        rows_low[t * TILE : (t + 1) * TILE, :] = values.astype(LOW)

    where_pair, where_panel = [], []
    for c in range(RADIX):
        low = c - pair_panel * pair_slots
        where_pair.append(jnp.where((low >= 0) & (low < pair_slots), low, junk))
        low = c - panel * panel_slots
        where_panel.append(jnp.where((low >= 0) & (low < panel_slots), low + pair_slots, junk))

    def forward(base, step):
        group, here = step % n_groups, pl.ds(base, TILE)
        spectra[step % 2] = jnp.dot(
            rows2[here, :], high_table[group], preferred_element_type=jnp.float32
        ) + jnp.dot(rows_low[here, :], low_table[group], preferred_element_type=jnp.float32)

    def multiply(base, step):
        group = step % n_groups
        source = spectra.at[step % 2]
        target = products.at[step % 2]
        chunk = 32
        for r in range(0, TILE, chunk):
            third = cube[pl.ds(base + r, chunk), :]
            for side in range(2):
                a_re, a_im, b_re, b_im, c_re, c_im = [
                    source[r : r + chunk, i * WIDE + side * HALF : i * WIDE + (side + 1) * HALF]
                    for i in range(6)
                ]
                a_re, a_im = a_re * third, a_im * third
                if group == 0 and side == 0:
                    real = a_re * b_re
                    both = a_im * b_im
                    m_re, m_im = real - both, a_re * b_im + a_im * b_re
                    first = lax.broadcasted_iota(jnp.int32, real.shape, 1) == 0
                    out_re = jnp.where(first, real * c_re, m_re * c_re - m_im * c_im)
                    out_im = jnp.where(first, both * c_im, m_re * c_im + m_im * c_re)
                else:
                    m_re, m_im = a_re * b_re - a_im * b_im, a_re * b_im + a_im * b_re
                    out_re = m_re * c_re - m_im * c_im
                    out_im = m_re * c_im + m_im * c_re
                if group == 0:
                    re_at, im_at = 2 * side * HALF, (2 * side + 1) * HALF
                else:
                    re_at, im_at = side * HALF, WIDE + side * HALF
                target[r : r + chunk, re_at : re_at + HALF] = out_re.astype(jnp.bfloat16)
                target[r : r + chunk, im_at : im_at + HALF] = out_im.astype(jnp.bfloat16)

    def inverse(step):
        group = step % n_groups
        source = products.at[step % 2]
        into = sums[step // n_groups]
        if group == 0:
            for side in range(2):
                at = slice(side * WIDE, (side + 1) * WIDE)
                into[:, at] = jnp.dot(source[:, at], ends_table[:, at], preferred_element_type=jnp.float32)
        else:
            into[:, 2 * group * WIDE : 2 * (group + 1) * WIDE] = jnp.dot(
                source[...], groups_table[group - 1], preferred_element_type=jnp.float32
            )

    def finish(source, base, part, parts):
        chunk = 16
        size = TILE // parts
        for r in range(part * size, (part + 1) * size, chunk):
            for side in range(2):
                outs = combine(
                    lambda i: source[r : r + chunk, i * WIDE + side * HALF : i * WIDE + (side + 1) * HALF]
                )
                at = slice(side * HALF, (side + 1) * HALF)
                for c in range(RADIX):
                    value = outs[c].astype(jnp.bfloat16)
                    kept[where_pair[c], pl.ds(base + r, chunk), at] = value
                    kept[where_panel[c], pl.ds(base + r, chunk), at] = value

    steps = 2 * n_groups

    def pair_step(t, _):
        bases = [pl.multiple_of(2 * t * TILE, TILE), pl.multiple_of((2 * t + 1) * TILE, TILE)]
        before = [pl.multiple_of(jnp.maximum(2 * t - 1, 1) * TILE, TILE), bases[0]]
        forward(bases[0], 0)
        for step in range(steps):
            if step + 1 < steps:
                forward(bases[(step + 1) // n_groups], step + 1)
            multiply(bases[step // n_groups], step)
            inverse(step)
            which = step // n_groups
            finish(sums[1 - which], before[which], step % n_groups, n_groups)
        return 0

    lax.fori_loop(0, rows // (2 * TILE), pair_step, 0)
    for part in range(n_groups):
        finish(sums[1], rows - TILE, part, n_groups)

    if not final:
        return
    odd = lax.rem(device, 2)
    each = pair_slots // 2
    marks = marks[:, : first + rows].astype(jnp.bfloat16)
    for i in range(each):
        for who, target in ((1 - odd, send_ref), (odd, own_ref)):
            left = kept[who * each + i].T
            left_early = early[who * each + i].T if first else None
            for j in range(panel_slots):
                block = jnp.dot(left, kept[pair_slots + j], preferred_element_type=jnp.float32)
                if first:
                    block += jnp.dot(left_early, early[pair_slots + j], preferred_element_type=jnp.float32)
                target[i * WIDE : (i + 1) * WIDE, j * WIDE : (j + 1) * WIDE] = block.astype(target.dtype)
    for j in range(panel_slots):
        line = jnp.dot(marks[:, first:], kept[pair_slots + j], preferred_element_type=jnp.float32)
        if first:
            line += jnp.dot(marks[:, :first], early[pair_slots + j], preferred_element_type=jnp.float32)
        at = slice(j * WIDE, (j + 1) * WIDE)
        own_ref[each * WIDE : each * WIDE + 8, at] = line
        send_ref[each * WIDE :, at] = jnp.concatenate([line, line], axis=0).astype(send_ref.dtype)


def merge_kernel(total, mine_ref, theirs_ref, mine_line_ref, theirs_line_ref, gram_ref, zty_ref):
    gram_ref[...] = (mine_ref[...] + theirs_ref[...].astype(jnp.float32)) * (1.0 / total)
    line = mine_line_ref[...] + theirs_line_ref[...].astype(jnp.float32)[:8]
    zty_ref[...] = line[:1] * total ** (-0.5)


def body(samples, targets, counts, bucket_ids, sign_bits):
    n_dp, n_feat = lax.axis_size("dp"), lax.axis_size("feat")
    slots, width = samples.shape
    half = slots // 2
    total = half * n_dp
    rows = total // 2
    scalars = [pl.BlockSpec(memory_space=pltpu.SMEM)]
    vector = pl.BlockSpec(memory_space=pltpu.VMEM)

    message = jax.ShapeDtypeStruct((half + PAD + TAIL, width), jnp.bfloat16)
    own, other = pl.pallas_call(
        prepare_kernel,
        out_shape=(message, message),
        in_specs=scalars + [vector] * 2,
        out_specs=(vector, vector),
    )(counts, samples, targets)

    def swap(block, bit):
        return lax.ppermute(block, "dp", [(i, i ^ bit) for i in range(n_dp)])

    high_table, low_table = forward_tables(bucket_ids, sign_bits)
    blocks = {0: own, 1: swap(other, 1)}
    near = [0, 1]
    for i in range(1, (n_dp - 1).bit_length()):
        for core in range(2):
            blocks[(1 << i) + core] = swap(other if core else own, (1 << i) + core)
            near.append((1 << i) + core)
    far = [delta for delta in range(n_dp) if delta not in blocks]
    sure = max(0, total - slots * len(far) - len(near)) // 2 if far else 0
    first = min(sure, rows // 3) // (2 * TILE) * 2 * TILE
    if first:
        high_table, sources = lax.optimization_barrier((high_table, dict(blocks)))
        blocks.update(sources)
    for delta in far:
        bits = [1 << i for i in range(1, n_dp.bit_length()) if delta >> i & 1]
        bit = bits[0] if delta % 2 else bits[-1]
        blocks[delta] = swap(blocks[delta ^ bit], bit)

    ends_table, group_table = inverse_tables()
    tables = (high_table, low_table, jnp.asarray(ends_table), jnp.asarray(group_table))
    own_columns, panel_columns = SK // n_dp, SK // n_feat
    kept_slots = 2 * own_columns // WIDE + panel_columns // WIDE + 1
    span = -(-(rows + half + 2 * PAD + 8) // 128) * 128

    def transform(deltas, begin, end, final, more):
        size = end - begin
        kept = (kept_slots, size, WIDE)
        out_shape = jax.ShapeDtypeStruct(kept, jnp.bfloat16)
        if final:
            out_shape = (
                jax.ShapeDtypeStruct((own_columns + 8, panel_columns), jnp.float32),
                jax.ShapeDtypeStruct((own_columns + 16, panel_columns), jnp.bfloat16),
            )
        scratch = [
            pltpu.SMEM((n_dp,), jnp.int32),
            pltpu.VMEM((span, width), jnp.float32),
            pltpu.VMEM((size, width), jnp.bfloat16),
            pltpu.VMEM((size, width), LOW),
            pltpu.VMEM((size, 128), jnp.float32),
            pltpu.VMEM((2, TILE, 6 * WIDE), jnp.float32),
            pltpu.VMEM((2, TILE, 2 * WIDE), jnp.bfloat16),
            pltpu.VMEM((TILE, SK), jnp.float32),
            pltpu.VMEM((TILE, SK), jnp.float32),
        ]
        return pl.pallas_call(
            functools.partial(main_kernel, deltas, begin, final),
            out_shape=out_shape,
            in_specs=scalars + [vector] * (len(deltas) + 4 + len(more)),
            out_specs=(vector, vector) if final else vector,
            scratch_shapes=scratch + ([pltpu.VMEM(kept, jnp.bfloat16)] if final else []),
            compiler_params=pltpu.CompilerParams(vmem_limit_bytes=VMEM_BYTES),
            cost_estimate=pl.CostEstimate(
                flops=2 * 10**7 * size, bytes_accessed=24 * 10**6, transcendentals=0
            ),
        )(counts, *[blocks[delta] for delta in deltas], *tables, *more)

    early = (transform(near, 0, first, False, ()),) if first else ()
    mine, send = transform(near + far, first, rows, True, early)
    theirs = swap(send, 1)
    blocks_in = min(own_columns, 2 * HALF)
    parts = own_columns // blocks_in
    rest = own_columns // 16
    gram, zty = pl.pallas_call(
        functools.partial(merge_kernel, total),
        grid=(parts,),
        out_shape=(
            jax.ShapeDtypeStruct((own_columns, panel_columns), jnp.float32),
            jax.ShapeDtypeStruct((1, panel_columns), jnp.float32),
        ),
        in_specs=[
            pl.BlockSpec((blocks_in, panel_columns), lambda i: (i, 0)),
            pl.BlockSpec((blocks_in, panel_columns), lambda i: (i, 0)),
            pl.BlockSpec((8, panel_columns), lambda i: (2 * rest, 0)),
            pl.BlockSpec((16, panel_columns), lambda i: (rest, 0)),
        ],
        out_specs=(
            pl.BlockSpec((blocks_in, panel_columns), lambda i: (i, 0)),
            pl.BlockSpec((1, panel_columns), lambda i: (0, 0)),
        ),
        compiler_params=pltpu.CompilerParams(vmem_limit_bytes=VMEM_BYTES // 2),
    )(mine, theirs, mine, theirs)
    return gram, zty.reshape(panel_columns)


def solution(mesh):
    placed = (P("dp", None), P("dp"), P(), P(), P())
    return jax.shard_map(
        body, mesh=mesh, in_specs=placed, out_specs=(P("dp", "feat"), P("feat")), check_vma=False
    )
```
